32 devices in a mesh: blk: 8 (over z, x), walk: 4 (over y, core).
Axes of the slice: x: 2, y: 2, z: 4, core: 2. Of those that a mesh axis runs over, the one named last changes fastest.
Arguments:
- green_half: bfloat16 [32, 50, 200], P(('blk', 'walk')), may hold values from -6 to 6
- chol_half: bfloat16 [600, 50, 200], P('blk'), may hold values from -0.0023956299 to 0.0023956299
- one_body: float32 [50, 200], replicated, may hold values from -0.06 to 0.06
- field_noise: float32 [32, 600], P(('blk', 'walk')), may hold values from -6 to 6
- old_weight: float32 [32], P(('blk', 'walk')), may hold values from 0.5 to 2
Outputs:
- force_bias: float32 [32, 600], P(('blk', 'walk'))
- energy: float32 [32], P(('blk', 'walk'))
- new_weight: float32 [32], P(('blk', 'walk'))
- comb_offset: float32 [32], P(('blk', 'walk'))
The draws below stay inside these ranges and needn't reach their ends.
All inputs are finite; a program needn't handle non-finite values.
Results may differ from the reference program's by a relative error of at most 0.00045.
Values may be sent and summed in bfloat16 or wider, within the bound.
No kernel may reach another device: no remote copies, remote signals or barrier semaphores. Data moves between devices by JAX's collectives and lax.ppermute only.
A program may use at most 64 MiB of HBM per device.

```python
import math
import jax
import jax.numpy as jnp
from jax import lax

M = 200
NOCC = 50
NCHOL = 600
WALKERS = 32


def shard_levels(stream_key, dims, split, smallest, top_value):
    factor_of = 1.0
    for dim, parts in split:
        heights = jax.random.uniform(jax.random.fold_in(jax.random.fold_in(stream_key, 6), dim), (parts,), jnp.float32, smallest / len(split), top_value / len(split))
        factor_of = factor_of * jnp.repeat(jnp.exp(heights), dims[dim] // parts).reshape((-1,) + (1,) * (len(dims) - 1 - dim))
    return factor_of


def centred(own_key, extent, width, bound, cuts=(), dtype=jnp.bfloat16):
    values = width * jax.random.normal(own_key, extent, jnp.float32)
    if cuts:
        values = values * shard_levels(own_key, extent, cuts, -0.22, 0.18)
    return jnp.clip(values, -bound, bound).astype(dtype)


def setup_inputs(seed: int = 0) -> dict:
    key_list = jax.random.split(jax.random.key(seed), 6)
    green_half = centred(key_list[0], (WALKERS, NOCC, M), 1.0, 6.0, ((0, 32),))
    chol_half = centred(key_list[1], (NCHOL, NOCC, M), 0.0004, 0.0023956299, ((0, 8),))
    one_body = centred(key_list[2], (NOCC, M), 0.01, 0.06, (), jnp.float32)
    field_noise = centred(key_list[3], (WALKERS, NCHOL), 1.0, 6.0, ((0, 32),), jnp.float32)
    old_weight = jnp.clip(jnp.exp(math.log(2.0) - 1.3862944 * jax.random.uniform(key_list[4], (WALKERS,), jnp.float32) ** shard_levels(key_list[4], (WALKERS,), ((0, 32),), -0.2, 0.2)), 0.5, 2.0)
    return {"green_half": green_half, "chol_half": chol_half, "one_body": one_body, "field_noise": field_noise, "old_weight": old_weight}


def reference(green_half, chol_half, one_body, field_noise, old_weight):
    orbitals = chol_half.shape[2]
    occupied = chol_half.shape[1]
    flat_slab = chol_half.astype(jnp.float32).reshape(-1, orbitals)

    def single(walker):
        table = jnp.dot(flat_slab, walker.astype(jnp.float32).T, precision=lax.Precision.HIGHEST)
        table = table.reshape(-1, occupied, occupied)
        traces = jnp.trace(table, axis1=1, axis2=2)
        crossed = jnp.sum(table * jnp.swapaxes(table, 1, 2), axis=(1, 2))
        return traces, crossed

    force_bias, crossed = lax.map(single, green_half)
    crossed_total = jnp.sum(crossed, axis=1)
    kinetic = jnp.sum(green_half.astype(jnp.float32) * one_body, axis=(1, 2))
    coulomb = 0.5 * jnp.sum(force_bias * force_bias, axis=1)
    energy = kinetic + coulomb - 0.5 * crossed_total
    shifted = jnp.float32(-0.1) * force_bias
    importance = jnp.sum(field_noise * shifted + 0.5 * shifted * shifted, axis=1)
    new_weight = old_weight * jnp.exp(importance - 0.01 * energy)
    before = jnp.cumsum(new_weight) - new_weight
    comb_offset = before * WALKERS / jnp.sum(new_weight) - jnp.arange(WALKERS).astype(jnp.float32)
    return force_bias, energy, new_weight, comb_offset
```

```python
import functools

import jax
import jax.numpy as jnp
from jax import lax
from jax.experimental import pallas as pl
from jax.experimental.pallas import tpu as pltpu
from jax.sharding import PartitionSpec as P

F32 = jnp.float32
BF16 = jnp.bfloat16
LANES = 128
GROUP = 8


def round_up(value, unit):
    return -(-value // unit) * unit


def split_three(values):
    high = values.astype(BF16)
    rest = values - high.astype(F32)
    middle = rest.astype(BF16)
    low = (rest - middle.astype(F32)).astype(BF16)
    return high, middle, low


def pack_kernel(slab, green_ref, noise_ref, packed_ref):
    blocks, rows, orbitals = packed_ref.shape
    occupied = green_ref.shape[1]
    green = green_ref[0].astype(F32)
    noise = noise_ref[...]
    pad = jnp.zeros((rows - occupied, orbitals), F32)
    base = jnp.concatenate([green, pad], axis=0)
    row = lax.broadcasted_iota(jnp.int32, (rows, orbitals), 0)
    for block in range(blocks):
        piece = noise[:, block * slab : (block + 1) * slab]
        piece = jnp.concatenate([piece, jnp.zeros((1, orbitals - slab), F32)], axis=1)
        value = base
        for k, part in enumerate(split_three(piece)):
            value = jnp.where(row == occupied + k, part.astype(F32), value)
        packed_ref[block] = value.astype(BF16)


def work_kernel(slab, offsets, walk, arrived_ref, green_ref, chol_ref, body_ref, old_ref, send_ref, rows_ref, lhs_ref, rhs_ref, table_ref):
    blocks, rows, orbitals = arrived_ref.shape
    occupied = chol_ref.shape[0]
    pairs = occupied // 2
    folds = send_ref.shape[0] // (blocks * walk)
    wide = folds * LANES
    at_energy, at_exponent, at_old, at_kinetic = offsets
    chunks = [(low, min(low + LANES, orbitals)) for low in range(0, orbitals, LANES)]
    for i in range(occupied):
        rhs_ref[i // 2, (i % 2) * LANES : (i % 2) * LANES + slab, :] = chol_ref[i]
    force, cross, noise = [], [], []
    lane = lax.broadcasted_iota(jnp.int32, (GROUP, LANES), 1)
    for first in range(0, blocks, GROUP):
        for w in range(GROUP):
            for c, (low, high) in enumerate(chunks):
                rows_ref[c, w * rows : (w + 1) * rows, : high - low] = arrived_ref[first + w, :, low:high].astype(F32)
        for j in range(0, occupied, 2):
            for c, (low, high) in enumerate(chunks):
                pair = [rows_ref[c, pl.ds(j + k, GROUP, stride=rows), :] for k in range(2)]
                pair = jnp.concatenate(pair, axis=0).astype(BF16)
                lhs_ref[j * GROUP : (j + 2) * GROUP, low:high] = pair[:, : high - low]
        parts = [rows_ref[0, pl.ds(occupied + k, GROUP, stride=rows), :] for k in range(3)]
        noise.append((parts[0] + parts[1]) + parts[2])
        lhs = lhs_ref[...]

        def fill(p, trace):
            product = lax.dot_general(lhs, rhs_ref[p], (((1,), (1,)), ((), ())), preferred_element_type=F32)
            table_ref[p] = product
            here = pl.multiple_of(p * 2 * GROUP, 2 * GROUP)
            both = table_ref[p, pl.ds(here, 2 * GROUP), :]
            return trace + both[:GROUP, :LANES] + both[GROUP:, LANES:]

        trace = lax.fori_loop(0, pairs, fill, jnp.zeros((GROUP, LANES), F32))

        def exchange(p, total):
            here = pl.multiple_of(p * 2 * GROUP, 2 * GROUP)
            for q in range(pairs):
                mine = table_ref[p, q * 2 * GROUP : (q + 1) * 2 * GROUP, :]
                other = table_ref[q, pl.ds(here, 2 * GROUP), :]
                total = total + mine[:GROUP, :LANES] * other[:GROUP, :LANES]
                total = total + mine[:GROUP, LANES:] * other[GROUP:, :LANES]
                total = total + mine[GROUP:, :LANES] * other[:GROUP, LANES:]
                total = total + mine[GROUP:, LANES:] * other[GROUP:, LANES:]
            return total

        total = lax.fori_loop(0, pairs, exchange, jnp.zeros((GROUP, LANES), F32))
        force.append(jnp.where(lane < slab, trace, 0.0))
        cross.append(jnp.where(lane < slab, total, 0.0))
    force = jnp.concatenate(force, axis=0)
    cross = jnp.concatenate(cross, axis=0)
    noise = jnp.concatenate(noise, axis=0)
    in_slab = lax.broadcasted_iota(jnp.int32, (blocks, LANES), 1) < slab
    shifted = F32(-0.1) * force
    gain = jnp.where(in_slab, noise * shifted + 0.5 * shifted * shifted, 0.0)
    energy = jnp.sum(0.5 * force * force - 0.5 * cross, axis=1, keepdims=True)
    exponent = jnp.sum(gain, axis=1, keepdims=True) - 0.01 * energy
    kinetic = jnp.sum(green_ref[0].astype(F32) * body_ref[...])
    old = old_ref[0]
    if wide > LANES:
        force = jnp.concatenate([force, jnp.zeros((blocks, wide - LANES), F32)], axis=1)
    lane = lax.broadcasted_iota(jnp.int32, (blocks, wide), 1)
    row = lax.broadcasted_iota(jnp.int32, (blocks, wide), 0)
    across = jnp.sum(jnp.where(lane - at_exponent == row, exponent, 0.0), axis=0, keepdims=True)
    message = jnp.where(lane < at_energy, force, energy)
    message = jnp.where(lane >= at_exponent, across, message)
    message = jnp.where(lane >= at_old, old, message)
    message = jnp.where(lane >= at_kinetic, kinetic, message)
    for k in range(walk * folds):
        c = k % folds
        send_ref[pl.ds(k, blocks, stride=walk * folds), :] = message[:, c * LANES : (c + 1) * LANES]


def finish_kernel(slab, offsets, blocks, walk, got_ref, force_ref, energy_ref, weight_ref, comb_ref):
    folds = got_ref.shape[0] // (blocks * walk)
    wide = folds * LANES
    at_energy, at_exponent, at_old, at_kinetic = offsets
    own_block = lax.axis_index("blk")
    own_walk = lax.axis_index("walk")
    lane = lax.broadcasted_iota(jnp.int32, (blocks, wide), 1)
    row = lax.broadcasted_iota(jnp.int32, (blocks, wide), 0)
    keep = (lane < at_old) | (lane - at_old == row) | (lane - at_kinetic == row)
    own = jnp.zeros((blocks, wide), F32)
    sums = []
    for w in range(walk):
        from_w = [got_ref[pl.ds(w * folds + c, blocks, stride=walk * folds), :] for c in range(folds)]
        from_w = jnp.concatenate(from_w, axis=1)
        own = jnp.where(own_walk == w, from_w, own)
        sums.append(jnp.sum(jnp.where(keep, from_w, 0.0), axis=0, keepdims=True))
    for b in range(blocks):
        force_ref[:, b * slab : (b + 1) * slab] = own[b : b + 1, :slab]
    sums = jnp.concatenate(sums, axis=0)
    exponent = sums[:, at_exponent : at_exponent + blocks]
    old = sums[:, at_old : at_old + blocks]
    kinetic = sums[:, at_kinetic : at_kinetic + blocks]
    weight = old * jnp.exp(exponent - 0.01 * kinetic)
    index = lax.broadcasted_iota(jnp.int32, (walk, blocks), 1) * walk + lax.broadcasted_iota(jnp.int32, (walk, blocks), 0)
    rank = own_block * walk + own_walk
    before = jnp.sum(jnp.where(index < rank, weight, 0.0))
    grand = jnp.sum(weight)
    weight_ref[0] = jnp.sum(jnp.where(index == rank, weight, 0.0))
    energy_ref[0] = jnp.sum(jnp.where(lane == at_energy, own, 0.0)) + jnp.sum(jnp.where(index == rank, kinetic, 0.0))
    comb_ref[0] = before * (blocks * walk) / grand - rank.astype(F32)


def on_device(green_half, chol_half, one_body, field_noise, old_weight):
    slab, occupied, orbitals = chol_half.shape
    blocks = lax.axis_size("blk")
    walk = lax.axis_size("walk")
    vmem = pl.BlockSpec(memory_space=pltpu.VMEM)
    smem = pl.BlockSpec(memory_space=pltpu.SMEM)
    rows = round_up(occupied + 3, 8)
    packed = pl.pallas_call(
        functools.partial(pack_kernel, slab),
        out_shape=jax.ShapeDtypeStruct((blocks, rows, orbitals), BF16),
        in_specs=[vmem, vmem],
        out_specs=vmem,
        name="pack",
    )(green_half, field_noise)
    arrived = lax.all_to_all(packed, "blk", split_axis=0, concat_axis=0, tiled=True)
    offsets = (slab, slab + 1, slab + 1 + blocks, slab + 1 + 2 * blocks)
    folds = round_up(slab + 1 + 3 * blocks, LANES) // LANES
    send = pl.pallas_call(
        functools.partial(work_kernel, slab, offsets, walk),
        out_shape=jax.ShapeDtypeStruct((blocks * walk * folds, LANES), F32),
        in_specs=[vmem, vmem, vmem, vmem, smem],
        out_specs=vmem,
        scratch_shapes=[
            pltpu.VMEM((round_up(orbitals, LANES) // LANES, GROUP * rows, LANES), F32),
            pltpu.VMEM((GROUP * occupied, orbitals), BF16),
            pltpu.VMEM((occupied // 2, 2 * LANES, orbitals), BF16),
            pltpu.VMEM((occupied // 2, GROUP * occupied, 2 * LANES), F32),
        ],
        compiler_params=pltpu.CompilerParams(vmem_limit_bytes=40 * 2**20),
        name="work",
    )(arrived, green_half, jnp.swapaxes(chol_half, 0, 1), one_body, old_weight)
    got = lax.all_to_all(send, ("blk", "walk"), split_axis=0, concat_axis=0, tiled=True)
    scalar = jax.ShapeDtypeStruct((1,), F32)
    return tuple(
        pl.pallas_call(
            functools.partial(finish_kernel, slab, offsets, blocks, walk),
            out_shape=(jax.ShapeDtypeStruct((1, slab * blocks), F32), scalar, scalar, scalar),
            in_specs=[vmem],
            out_specs=(vmem, smem, smem, smem),
            name="finish",
        )(got)
    )


def solution(mesh):
    placed = (
        P(("blk", "walk"), None, None),
        P("blk", None, None),
        P(),
        P(("blk", "walk"), None),
        P(("blk", "walk")),
    )
    return jax.shard_map(
        on_device,
        mesh=mesh,
        in_specs=placed,
        out_specs=(
            P(("blk", "walk"), None),
            P(("blk", "walk")),
            P(("blk", "walk")),
            P(("blk", "walk")),
        ),
        check_vma=False,
    )
```

```python
import functools

import jax
import jax.numpy as jnp
from jax import lax
from jax.experimental import pallas as pl
from jax.experimental.pallas import tpu as pltpu
from jax.sharding import PartitionSpec as P

F32 = jnp.float32
BF16 = jnp.bfloat16
LANES = 128
GROUP = 8


def round_up(value, unit):
    return -(-value // unit) * unit


def split_three(values):
    high = values.astype(BF16)
    rest = values - high.astype(F32)
    middle = rest.astype(BF16)
    low = (rest - middle.astype(F32)).astype(BF16)
    return high, middle, low


def pack_kernel(slab, green_ref, noise_ref, packed_ref):
    blocks, rows, orbitals = packed_ref.shape
    occupied = green_ref.shape[1]
    green = green_ref[0].astype(F32)
    noise = noise_ref[...]
    pad = jnp.zeros((rows - occupied, orbitals), F32)
    base = jnp.concatenate([green, pad], axis=0)
    row = lax.broadcasted_iota(jnp.int32, (rows, orbitals), 0)
    for block in range(blocks):
        piece = noise[:, block * slab : (block + 1) * slab]
        piece = jnp.concatenate([piece, jnp.zeros((1, orbitals - slab), F32)], axis=1)
        value = base
        for k, part in enumerate(split_three(piece)):
            value = jnp.where(row == occupied + k, part.astype(F32), value)
        packed_ref[block] = value.astype(BF16)


def prepare_kernel(slab, green_ref, chol_ref, body_ref, rhs_ref, kinetic_ref):
    for i in range(chol_ref.shape[0]):
        rhs_ref[i // 2, (i % 2) * LANES : (i % 2) * LANES + slab, :] = chol_ref[i]
    kinetic_ref[0] = jnp.sum(green_ref[0].astype(F32) * body_ref[...])


def tables_of(lhs, rhs_ref, table_ref):
    trace = [jnp.zeros((GROUP, LANES), F32) for _ in range(2)]
    twice = [jnp.zeros((GROUP, LANES), F32) for _ in range(4)]
    once = jnp.zeros((GROUP, LANES), F32)
    for p in range(rhs_ref.shape[0]):
        table_ref[p] = lax.dot_general(lhs, rhs_ref[p], (((1,), (1,)), ((), ())), preferred_element_type=F32)
        for q in range(p):
            mine = table_ref[p, q * 2 * GROUP : (q + 1) * 2 * GROUP, :]
            other = table_ref[q, p * 2 * GROUP : (p + 1) * 2 * GROUP, :]
            twice[0] += mine[:GROUP, :LANES] * other[:GROUP, :LANES]
            twice[1] += mine[:GROUP, LANES:] * other[GROUP:, :LANES]
            twice[2] += mine[GROUP:, :LANES] * other[:GROUP, LANES:]
            twice[3] += mine[GROUP:, LANES:] * other[GROUP:, LANES:]
        both = table_ref[p, p * 2 * GROUP : (p + 1) * 2 * GROUP, :]
        trace[0] += both[:GROUP, :LANES]
        trace[1] += both[GROUP:, LANES:]
        once += both[:GROUP, :LANES] * both[:GROUP, :LANES] + both[GROUP:, LANES:] * both[GROUP:, LANES:]
        twice[0] += both[:GROUP, LANES:] * both[GROUP:, :LANES]
    return trace[0] + trace[1], once + 2.0 * ((twice[0] + twice[1]) + (twice[2] + twice[3]))


def work_kernel(slab, offsets, walk, arrived_ref, rhs_ref, kinetic_ref, old_ref, send_ref, rows_ref, lhs_ref, table_ref):
    blocks, rows, orbitals = arrived_ref.shape
    occupied = lhs_ref.shape[0] // GROUP
    folds = send_ref.shape[0] // (blocks * walk)
    wide = folds * LANES
    at_energy, at_exponent, at_old, at_kinetic = offsets
    chunks = [(low, min(low + LANES, orbitals)) for low in range(0, orbitals, LANES)]
    force, cross, noise = [], [], []
    lane = lax.broadcasted_iota(jnp.int32, (GROUP, LANES), 1)
    for first in range(0, blocks, GROUP):
        for w in range(GROUP):
            for c, (low, high) in enumerate(chunks):
                rows_ref[c, w * rows : (w + 1) * rows, : high - low] = arrived_ref[first + w, :, low:high].astype(F32)
        for j in range(0, occupied, 2):
            for c, (low, high) in enumerate(chunks):
                pair = [rows_ref[c, pl.ds(j + k, GROUP, stride=rows), :] for k in range(2)]
                pair = jnp.concatenate(pair, axis=0).astype(BF16)
                lhs_ref[j * GROUP : (j + 2) * GROUP, low:high] = pair[:, : high - low]
        parts = [rows_ref[0, pl.ds(occupied + k, GROUP, stride=rows), :] for k in range(3)]
        noise.append((parts[0] + parts[1]) + parts[2])
        trace, total = tables_of(lhs_ref[...], rhs_ref, table_ref)
        force.append(jnp.where(lane < slab, trace, 0.0))
        cross.append(jnp.where(lane < slab, total, 0.0))
    force = jnp.concatenate(force, axis=0)
    cross = jnp.concatenate(cross, axis=0)
    noise = jnp.concatenate(noise, axis=0)
    in_slab = lax.broadcasted_iota(jnp.int32, (blocks, LANES), 1) < slab
    shifted = F32(-0.1) * force
    gain = jnp.where(in_slab, noise * shifted + 0.5 * shifted * shifted, 0.0)
    energy = jnp.sum(0.5 * force * force - 0.5 * cross, axis=1, keepdims=True)
    exponent = jnp.sum(gain, axis=1, keepdims=True) - 0.01 * energy
    if wide > LANES:
        force = jnp.concatenate([force, jnp.zeros((blocks, wide - LANES), F32)], axis=1)
    lane = lax.broadcasted_iota(jnp.int32, (blocks, wide), 1)
    row = lax.broadcasted_iota(jnp.int32, (blocks, wide), 0)
    across = jnp.sum(jnp.where(lane - at_exponent == row, exponent, 0.0), axis=0, keepdims=True)
    message = jnp.where(lane < at_energy, force, energy)
    message = jnp.where(lane >= at_exponent, across, message)
    message = jnp.where(lane >= at_old, old_ref[0], message)
    message = jnp.where(lane >= at_kinetic, kinetic_ref[0], message)
    for k in range(walk * folds):
        c = k % folds
        send_ref[pl.ds(k, blocks, stride=walk * folds), :] = message[:, c * LANES : (c + 1) * LANES]


def finish_kernel(slab, offsets, blocks, walk, got_ref, force_ref, energy_ref, weight_ref, comb_ref):
    folds = got_ref.shape[0] // (blocks * walk)
    wide = folds * LANES
    at_energy, at_exponent, at_old, at_kinetic = offsets
    own_block = lax.axis_index("blk")
    own_walk = lax.axis_index("walk")
    lane = lax.broadcasted_iota(jnp.int32, (blocks, wide), 1)
    row = lax.broadcasted_iota(jnp.int32, (blocks, wide), 0)
    keep = (lane < at_old) | (lane - at_old == row) | (lane - at_kinetic == row)
    own = jnp.zeros((blocks, wide), F32)
    sums = []
    for w in range(walk):
        from_w = [got_ref[pl.ds(w * folds + c, blocks, stride=walk * folds), :] for c in range(folds)]
        from_w = jnp.concatenate(from_w, axis=1)
        own = jnp.where(own_walk == w, from_w, own)
        sums.append(jnp.sum(jnp.where(keep, from_w, 0.0), axis=0, keepdims=True))
    for b in range(blocks):
        force_ref[:, b * slab : (b + 1) * slab] = own[b : b + 1, :slab]
    sums = jnp.concatenate(sums, axis=0)
    exponent = sums[:, at_exponent : at_exponent + blocks]
    old = sums[:, at_old : at_old + blocks]
    kinetic = sums[:, at_kinetic : at_kinetic + blocks]
    weight = old * jnp.exp(exponent - 0.01 * kinetic)
    index = lax.broadcasted_iota(jnp.int32, (walk, blocks), 1) * walk + lax.broadcasted_iota(jnp.int32, (walk, blocks), 0)
    rank = own_block * walk + own_walk
    before = jnp.sum(jnp.where(index < rank, weight, 0.0))
    grand = jnp.sum(weight)
    weight_ref[0] = jnp.sum(jnp.where(index == rank, weight, 0.0))
    energy_ref[0] = jnp.sum(jnp.where(lane == at_energy, own, 0.0)) + jnp.sum(jnp.where(index == rank, kinetic, 0.0))
    comb_ref[0] = before * (blocks * walk) / grand - rank.astype(F32)


def on_device(green_half, chol_half, one_body, field_noise, old_weight):
    slab, occupied, orbitals = chol_half.shape
    blocks = lax.axis_size("blk")
    walk = lax.axis_size("walk")
    vmem = pl.BlockSpec(memory_space=pltpu.VMEM)
    smem = pl.BlockSpec(memory_space=pltpu.SMEM)
    rows = round_up(occupied + 3, 8)
    pairs = occupied // 2
    small = pltpu.CompilerParams(vmem_limit_bytes=4 * 2**20)
    packed = pl.pallas_call(
        functools.partial(pack_kernel, slab),
        out_shape=jax.ShapeDtypeStruct((blocks, rows, orbitals), BF16),
        in_specs=[vmem, vmem],
        out_specs=vmem,
        compiler_params=small,
        name="pack",
    )(green_half, field_noise)
    arrived = lax.all_to_all(packed, "blk", split_axis=0, concat_axis=0, tiled=True)
    rhs, kinetic = pl.pallas_call(
        functools.partial(prepare_kernel, slab),
        out_shape=(
            jax.ShapeDtypeStruct((pairs, 2 * LANES, orbitals), BF16),
            jax.ShapeDtypeStruct((1,), F32),
        ),
        in_specs=[vmem, vmem, vmem],
        out_specs=(vmem, smem),
        compiler_params=pltpu.CompilerParams(vmem_limit_bytes=12 * 2**20),
        name="prepare",
    )(green_half, jnp.swapaxes(chol_half, 0, 1), one_body)
    offsets = (slab, slab + 1, slab + 1 + blocks, slab + 1 + 2 * blocks)
    folds = round_up(slab + 1 + 3 * blocks, LANES) // LANES
    send = pl.pallas_call(
        functools.partial(work_kernel, slab, offsets, walk),
        out_shape=jax.ShapeDtypeStruct((blocks * walk * folds, LANES), F32),
        in_specs=[vmem, vmem, smem, smem],
        out_specs=vmem,
        scratch_shapes=[
            pltpu.VMEM((round_up(orbitals, LANES) // LANES, GROUP * rows, LANES), F32),
            pltpu.VMEM((GROUP * occupied, orbitals), BF16),
            pltpu.VMEM((pairs, GROUP * occupied, 2 * LANES), F32),
        ],
        compiler_params=pltpu.CompilerParams(vmem_limit_bytes=32 * 2**20),
        name="work",
    )(arrived, rhs, kinetic, old_weight)
    got = lax.all_to_all(send, ("blk", "walk"), split_axis=0, concat_axis=0, tiled=True)
    scalar = jax.ShapeDtypeStruct((1,), F32)
    return tuple(
        pl.pallas_call(
            functools.partial(finish_kernel, slab, offsets, blocks, walk),
            out_shape=(jax.ShapeDtypeStruct((1, slab * blocks), F32), scalar, scalar, scalar),
            in_specs=[vmem],
            out_specs=(vmem, smem, smem, smem),
            compiler_params=small,
            name="finish",
        )(got)
    )


def solution(mesh):
    placed = (
        P(("blk", "walk"), None, None),
        P("blk", None, None),
        P(),
        P(("blk", "walk"), None),
        P(("blk", "walk")),
    )
    return jax.shard_map(
        on_device,
        mesh=mesh,
        in_specs=placed,
        out_specs=(
            P(("blk", "walk"), None),
            P(("blk", "walk")),
            P(("blk", "walk")),
            P(("blk", "walk")),
        ),
        check_vma=False,
    )
```

```python
import functools

import jax
import jax.numpy as jnp
from jax import lax
from jax.experimental import pallas as pl
from jax.experimental.pallas import tpu as pltpu
from jax.sharding import PartitionSpec as P

F32 = jnp.float32
BF16 = jnp.bfloat16
LANES = 128
TILE = 8
HALF = LANES // 2
GROUP = 8


def round_up(value, unit):
    return -(-value // unit) * unit


def split_three(values):
    high = values.astype(BF16)
    rest = values - high.astype(F32)
    middle = rest.astype(BF16)
    low = (rest - middle.astype(F32)).astype(BF16)
    return high, middle, low


def packed_rows(occupied):
    first = round_up(occupied + 3, TILE)
    return first, round_up(first + TILE, 2 * TILE) // 2


def pack_kernel(slab, green_hbm, noise_hbm, packed_hbm, green_ref, noise_ref, rest_ref, packed_ref, in_sems, out_sems):
    blocks = packed_ref.shape[0]
    _, occupied, orbitals = green_ref.shape
    first, second = packed_rows(occupied)
    copies = [
        pltpu.make_async_copy(green_hbm, green_ref, in_sems.at[0]),
        pltpu.make_async_copy(noise_hbm, noise_ref, in_sems.at[1]),
    ]
    for copy in copies:
        copy.start()
    rest_ref[...] = jnp.zeros_like(rest_ref)
    for copy in copies:
        copy.wait()
    rest_ref[:occupied, : orbitals - LANES] = green_ref[0, :, LANES:].astype(F32)
    tiles = [rest_ref[t : t + TILE, :] for t in range(0, first, TILE)]
    half = second // TILE
    lane = lax.broadcasted_iota(jnp.int32, (TILE, LANES), 1)
    row = lax.broadcasted_iota(jnp.int32, (TILE, LANES), 0)
    folded = [jnp.where(lane < HALF, tiles[t], pltpu.roll(tiles[t + half], HALF, 1)) for t in range(half - 1)]
    ends = tiles[half - 1]
    for t in range(len(tiles)):
        moved = pltpu.roll(tiles[t], t * TILE, 1) if t else tiles[t]
        ends = jnp.where((lane >= HALF + t * TILE) & (lane < HALF + (t + 1) * TILE), moved, ends)
    whole = green_ref[0, :, :LANES].astype(F32)
    cut = occupied // TILE * TILE
    tail = jnp.concatenate([whole[cut:], jnp.zeros((first - occupied, LANES), F32)], axis=0)
    noise = noise_ref[...]
    sends = []
    for block in range(blocks):
        piece = noise[:, block * slab : (block + 1) * slab]
        piece = jnp.concatenate([piece, jnp.zeros((1, LANES - slab), F32)], axis=1)
        last = tail
        for k, part in enumerate(split_three(piece)):
            last = jnp.where(row == occupied - cut + k, part.astype(F32), last)
        packed_ref[block] = jnp.concatenate([whole[:cut], last, *folded, ends], axis=0).astype(BF16)
        sends.append(pltpu.make_async_copy(packed_ref.at[block], packed_hbm.at[block], out_sems.at[block]))
        sends[-1].start()
    for send in sends:
        send.wait()


def unpack(packed, rows_ref, at, occupied):
    first, second = packed_rows(occupied)
    half = second // TILE
    rows_ref[0, at : at + first, :] = packed[:first]
    lane = lax.broadcasted_iota(jnp.int32, (TILE, LANES), 1)
    ends = packed[first + second - TILE :]
    for t in range(first // TILE):
        place = first + (t % half) * TILE
        tile = packed[place : place + TILE]
        tile = pltpu.roll(tile, HALF, 1) if t >= half else tile
        end = pltpu.roll(ends, LANES - t * TILE, 1) if t else ends
        rows_ref[1, at + t * TILE : at + (t + 1) * TILE, :] = jnp.where(lane < HALF, tile, end)


def prepare_kernel(slab, chol_ref, rhs_ref):
    for i in range(chol_ref.shape[0]):
        rhs_ref[i // 2, (i % 2) * LANES : (i % 2) * LANES + slab, :] = chol_ref[i]


def tables_of(lhs, rhs_ref, table_ref):
    trace = [jnp.zeros((GROUP, LANES), F32) for _ in range(2)]
    twice = [jnp.zeros((GROUP, LANES), F32) for _ in range(4)]
    once = jnp.zeros((GROUP, LANES), F32)
    for p in range(rhs_ref.shape[0]):
        table_ref[p] = lax.dot_general(lhs, rhs_ref[p], (((1,), (1,)), ((), ())), preferred_element_type=F32)
        for q in range(p):
            mine = table_ref[p, q * 2 * GROUP : (q + 1) * 2 * GROUP, :]
            other = table_ref[q, p * 2 * GROUP : (p + 1) * 2 * GROUP, :]
            twice[0] += mine[:GROUP, :LANES] * other[:GROUP, :LANES]
            twice[1] += mine[:GROUP, LANES:] * other[GROUP:, :LANES]
            twice[2] += mine[GROUP:, :LANES] * other[:GROUP, LANES:]
            twice[3] += mine[GROUP:, LANES:] * other[GROUP:, LANES:]
        both = table_ref[p, p * 2 * GROUP : (p + 1) * 2 * GROUP, :]
        trace[0] += both[:GROUP, :LANES]
        trace[1] += both[GROUP:, LANES:]
        once += both[:GROUP, :LANES] * both[:GROUP, :LANES] + both[GROUP:, LANES:] * both[GROUP:, LANES:]
        twice[0] += both[:GROUP, LANES:] * both[GROUP:, :LANES]
    return trace[0] + trace[1], once + 2.0 * ((twice[0] + twice[1]) + (twice[2] + twice[3]))


def work_kernel(slab, offsets, walk, arrived_ref, rhs_ref, body_ref, old_ref, send_ref, rows_ref, lhs_ref, table_ref):
    blocks = arrived_ref.shape[0]
    occupied, orbitals = body_ref.shape
    rows, _ = packed_rows(occupied)
    folds = send_ref.shape[0] // (blocks * walk)
    wide = folds * LANES
    at_energy, at_exponent, at_old, at_kinetic = offsets
    chunks = [(low, min(low + LANES, orbitals)) for low in range(0, orbitals, LANES)]
    own = lax.axis_index("blk")
    kinetic = jnp.zeros((1, 1), F32)
    force, cross, noise = [], [], []
    lane = lax.broadcasted_iota(jnp.int32, (GROUP, LANES), 1)
    for first in range(0, blocks, GROUP):
        for w in range(GROUP):
            unpack(arrived_ref[first + w].astype(F32), rows_ref, w * rows, occupied)
        for j in range(0, occupied, 2):
            for c, (low, high) in enumerate(chunks):
                pair = [rows_ref[c, pl.ds(j + k, GROUP, stride=rows), :] for k in range(2)]
                pair = jnp.concatenate(pair, axis=0).astype(BF16)
                lhs_ref[j * GROUP : (j + 2) * GROUP, low:high] = pair[:, : high - low]
        place = pl.multiple_of(lax.rem(own, GROUP) * rows, TILE)
        here = jnp.zeros((1, 1), F32)
        for c, (low, high) in enumerate(chunks):
            mine = rows_ref[c, pl.ds(place, occupied), :][:, : high - low]
            here += jnp.sum(mine * body_ref[:, low:high], axis=(0, 1), keepdims=True)
        kinetic = jnp.where(own // GROUP == first // GROUP, here, kinetic)
        parts = [rows_ref[0, pl.ds(occupied + k, GROUP, stride=rows), :] for k in range(3)]
        noise.append((parts[0] + parts[1]) + parts[2])
        trace, total = tables_of(lhs_ref[...], rhs_ref, table_ref)
        force.append(jnp.where(lane < slab, trace, 0.0))
        cross.append(jnp.where(lane < slab, total, 0.0))
    force = jnp.concatenate(force, axis=0)
    cross = jnp.concatenate(cross, axis=0)
    noise = jnp.concatenate(noise, axis=0)
    in_slab = lax.broadcasted_iota(jnp.int32, (blocks, LANES), 1) < slab
    shifted = F32(-0.1) * force
    gain = jnp.where(in_slab, noise * shifted + 0.5 * shifted * shifted, 0.0)
    energy = jnp.sum(0.5 * force * force - 0.5 * cross, axis=1, keepdims=True)
    exponent = jnp.sum(gain, axis=1, keepdims=True) - 0.01 * energy
    if wide > LANES:
        force = jnp.concatenate([force, jnp.zeros((blocks, wide - LANES), F32)], axis=1)
    lane = lax.broadcasted_iota(jnp.int32, (blocks, wide), 1)
    row = lax.broadcasted_iota(jnp.int32, (blocks, wide), 0)
    across = jnp.sum(jnp.where(lane - at_exponent == row, exponent, 0.0), axis=0, keepdims=True)
    message = jnp.where(lane < at_energy, force, energy)
    message = jnp.where(lane >= at_exponent, across, message)
    message = jnp.where(lane >= at_old, old_ref[...], message)
    message = jnp.where(lane >= at_kinetic, kinetic, message)
    for k in range(walk * folds):
        c = k % folds
        send_ref[pl.ds(k, blocks, stride=walk * folds), :] = message[:, c * LANES : (c + 1) * LANES]


def finish_kernel(slab, offsets, blocks, walk, got_ref, force_ref, energy_ref, weight_ref, comb_ref):
    folds = got_ref.shape[0] // (blocks * walk)
    wide = folds * LANES
    at_energy, at_exponent, at_old, at_kinetic = offsets
    own_block = lax.axis_index("blk")
    own_walk = lax.axis_index("walk")
    lane = lax.broadcasted_iota(jnp.int32, (blocks, wide), 1)
    row = lax.broadcasted_iota(jnp.int32, (blocks, wide), 0)
    keep = (lane < at_old) | (lane - at_old == row) | (lane - at_kinetic == row)
    own = jnp.zeros((blocks, wide), F32)
    sums = []
    for w in range(walk):
        from_w = [got_ref[pl.ds(w * folds + c, blocks, stride=walk * folds), :] for c in range(folds)]
        from_w = jnp.concatenate(from_w, axis=1)
        own = jnp.where(own_walk == w, from_w, own)
        sums.append(jnp.sum(jnp.where(keep, from_w, 0.0), axis=0, keepdims=True))
    for b in range(blocks):
        force_ref[:, b * slab : (b + 1) * slab] = own[b : b + 1, :slab]
    sums = jnp.concatenate(sums, axis=0)
    exponent = sums[:, at_exponent : at_exponent + blocks]
    old = sums[:, at_old : at_old + blocks]
    kinetic = sums[:, at_kinetic : at_kinetic + blocks]
    weight = old * jnp.exp(exponent - 0.01 * kinetic)
    index = lax.broadcasted_iota(jnp.int32, (walk, blocks), 1) * walk + lax.broadcasted_iota(jnp.int32, (walk, blocks), 0)
    rank = own_block * walk + own_walk

    def total(values):
        return jnp.sum(values, axis=(0, 1), keepdims=True)

    before = total(jnp.where(index < rank, weight, 0.0))
    weight_ref[...] = total(jnp.where(index == rank, weight, 0.0))
    energy_ref[...] = total(jnp.where(lane == at_energy, own, 0.0)) + total(jnp.where(index == rank, kinetic, 0.0))
    comb_ref[...] = before * (blocks * walk) / total(weight) - rank.astype(F32)


def on_device(green_half, chol_half, one_body, field_noise, old_weight):
    slab, occupied, orbitals = chol_half.shape
    blocks = lax.axis_size("blk")
    walk = lax.axis_size("walk")
    vmem = pl.BlockSpec(memory_space=pltpu.VMEM)
    hbm = pl.BlockSpec(memory_space=pltpu.HBM)
    first, second = packed_rows(occupied)
    pairs = occupied // 2
    small = pltpu.CompilerParams(vmem_limit_bytes=4 * 2**20)
    message = (blocks, first + second, LANES)
    packed = pl.pallas_call(
        functools.partial(pack_kernel, slab),
        out_shape=jax.ShapeDtypeStruct(message, BF16),
        in_specs=[hbm, hbm],
        out_specs=hbm,
        scratch_shapes=[
            pltpu.VMEM(green_half.shape, BF16),
            pltpu.VMEM(field_noise.shape, F32),
            pltpu.VMEM((first, LANES), F32),
            pltpu.VMEM(message, BF16),
            pltpu.SemaphoreType.DMA((2,)),
            pltpu.SemaphoreType.DMA((blocks,)),
        ],
        compiler_params=pltpu.CompilerParams(vmem_limit_bytes=60 * 2**20),
        name="pack",
    )(green_half, field_noise)
    arrived = lax.all_to_all(packed, "blk", split_axis=0, concat_axis=0, tiled=True)
    rhs = pl.pallas_call(
        functools.partial(prepare_kernel, slab),
        out_shape=jax.ShapeDtypeStruct((pairs, 2 * LANES, orbitals), BF16),
        in_specs=[vmem],
        out_specs=vmem,
        compiler_params=pltpu.CompilerParams(vmem_limit_bytes=12 * 2**20),
        name="prepare",
    )(jnp.swapaxes(chol_half, 0, 1))
    offsets = (slab, slab + 1, slab + 1 + blocks, slab + 1 + 2 * blocks)
    folds = round_up(slab + 1 + 3 * blocks, LANES) // LANES
    send = pl.pallas_call(
        functools.partial(work_kernel, slab, offsets, walk),
        out_shape=jax.ShapeDtypeStruct((blocks * walk * folds, LANES), F32),
        in_specs=[vmem] * 4,
        out_specs=vmem,
        scratch_shapes=[
            pltpu.VMEM((round_up(orbitals, LANES) // LANES, GROUP * first, LANES), F32),
            pltpu.VMEM((GROUP * occupied, orbitals), BF16),
            pltpu.VMEM((pairs, GROUP * occupied, 2 * LANES), F32),
        ],
        compiler_params=pltpu.CompilerParams(vmem_limit_bytes=32 * 2**20),
        name="work",
    )(arrived, rhs, one_body, old_weight.reshape(1, 1))
    got = lax.all_to_all(send, ("blk", "walk"), split_axis=0, concat_axis=0, tiled=True)
    one = jax.ShapeDtypeStruct((1, 1), F32)
    force, energy, weight, comb = pl.pallas_call(
        functools.partial(finish_kernel, slab, offsets, blocks, walk),
        out_shape=(jax.ShapeDtypeStruct((1, slab * blocks), F32), one, one, one),
        in_specs=[vmem],
        out_specs=(vmem,) * 4,
        compiler_params=small,
        name="finish",
    )(got)
    return force, energy.reshape(1), weight.reshape(1), comb.reshape(1)


def solution(mesh):
    placed = (
        P(("blk", "walk"), None, None),
        P("blk", None, None),
        P(),
        P(("blk", "walk"), None),
        P(("blk", "walk")),
    )
    return jax.shard_map(
        on_device,
        mesh=mesh,
        in_specs=placed,
        out_specs=(
            P(("blk", "walk"), None),
            P(("blk", "walk")),
            P(("blk", "walk")),
            P(("blk", "walk")),
        ),
        check_vma=False,
    )
```

```python
import functools

import jax
import jax.numpy as jnp
from jax import lax
from jax.experimental import pallas as pl
from jax.experimental.pallas import tpu as pltpu
from jax.sharding import PartitionSpec as P

F32 = jnp.float32
BF16 = jnp.bfloat16
LANES = 128
TILE = 8
HALF = LANES // 2
GROUP = 8


def round_up(value, unit):
    return -(-value // unit) * unit


def split_three(values):
    high = values.astype(BF16)
    rest = values - high.astype(F32)
    middle = rest.astype(BF16)
    low = (rest - middle.astype(F32)).astype(BF16)
    return high, middle, low


def exchange_order(blocks):
    if blocks % 4:
        return list(range(blocks))
    lines = blocks // 2
    line = [z for pair in zip(range(lines // 2 - 1, -1, -1), range(lines - 1, lines // 2 - 1, -1)) for z in pair]
    return [2 * z + x for x in (1, 0) for z in line]


def packed_rows(occupied):
    first = round_up(occupied + 3, TILE)
    return first, round_up(first + TILE, 2 * TILE) // 2


def pack_kernel(slab, order, green_hbm, noise_hbm, packed_hbm, green_ref, noise_ref, rest_ref, packed_ref, in_sems, out_sems):
    _, occupied, orbitals = green_ref.shape
    first, second = packed_rows(occupied)
    copies = [
        pltpu.make_async_copy(green_hbm, green_ref, in_sems.at[0]),
        pltpu.make_async_copy(noise_hbm, noise_ref, in_sems.at[1]),
    ]
    for copy in copies:
        copy.start()
    rest_ref[...] = jnp.zeros_like(rest_ref)
    for copy in copies:
        copy.wait()
    rest_ref[:occupied, : orbitals - LANES] = green_ref[0, :, LANES:].astype(F32)
    tiles = [rest_ref[t : t + TILE, :] for t in range(0, first, TILE)]
    half = second // TILE
    lane = lax.broadcasted_iota(jnp.int32, (TILE, LANES), 1)
    row = lax.broadcasted_iota(jnp.int32, (TILE, LANES), 0)
    folded = [jnp.where(lane < HALF, tiles[t], pltpu.roll(tiles[t + half], HALF, 1)) for t in range(half - 1)]
    ends = tiles[half - 1]
    for t in range(len(tiles)):
        moved = pltpu.roll(tiles[t], t * TILE, 1) if t else tiles[t]
        ends = jnp.where((lane >= HALF + t * TILE) & (lane < HALF + (t + 1) * TILE), moved, ends)
    whole = green_ref[0, :, :LANES].astype(F32)
    cut = occupied // TILE * TILE
    tail = jnp.concatenate([whole[cut:], jnp.zeros((first - occupied, LANES), F32)], axis=0)
    noise = noise_ref[...]
    sends = []
    for slot, block in enumerate(order):
        piece = noise[:, block * slab : (block + 1) * slab]
        piece = jnp.concatenate([piece, jnp.zeros((1, LANES - slab), F32)], axis=1)
        last = tail
        for k, part in enumerate(split_three(piece)):
            last = jnp.where(row == occupied - cut + k, part.astype(F32), last)
        packed_ref[slot] = jnp.concatenate([whole[:cut], last, *folded, ends], axis=0).astype(BF16)
        sends.append(pltpu.make_async_copy(packed_ref.at[slot], packed_hbm.at[slot], out_sems.at[slot]))
        sends[-1].start()
    for send in sends:
        send.wait()


def unpack(packed, rows_ref, at, occupied):
    first, second = packed_rows(occupied)
    half = second // TILE
    rows_ref[0, at : at + first, :] = packed[:first]
    lane = lax.broadcasted_iota(jnp.int32, (TILE, LANES), 1)
    ends = packed[first + second - TILE :]
    for t in range(first // TILE):
        place = first + (t % half) * TILE
        tile = packed[place : place + TILE]
        tile = pltpu.roll(tile, HALF, 1) if t >= half else tile
        end = pltpu.roll(ends, LANES - t * TILE, 1) if t else ends
        rows_ref[1, at + t * TILE : at + (t + 1) * TILE, :] = jnp.where(lane < HALF, tile, end)


def prepare_kernel(slab, chol_ref, rhs_ref):
    for i in range(chol_ref.shape[0]):
        rhs_ref[i // 2, (i % 2) * LANES : (i % 2) * LANES + slab, :] = chol_ref[i]


def tables_of(lhs, rhs_ref, table_ref):
    trace = [jnp.zeros((GROUP, LANES), F32) for _ in range(2)]
    twice = [jnp.zeros((GROUP, LANES), F32) for _ in range(4)]
    once = jnp.zeros((GROUP, LANES), F32)
    for p in range(rhs_ref.shape[0]):
        table_ref[p] = lax.dot_general(lhs, rhs_ref[p], (((1,), (1,)), ((), ())), preferred_element_type=F32)
        for q in range(p):
            mine = table_ref[p, q * 2 * GROUP : (q + 1) * 2 * GROUP, :]
            other = table_ref[q, p * 2 * GROUP : (p + 1) * 2 * GROUP, :]
            twice[0] += mine[:GROUP, :LANES] * other[:GROUP, :LANES]
            twice[1] += mine[:GROUP, LANES:] * other[GROUP:, :LANES]
            twice[2] += mine[GROUP:, :LANES] * other[:GROUP, LANES:]
            twice[3] += mine[GROUP:, LANES:] * other[GROUP:, LANES:]
        both = table_ref[p, p * 2 * GROUP : (p + 1) * 2 * GROUP, :]
        trace[0] += both[:GROUP, :LANES]
        trace[1] += both[GROUP:, LANES:]
        once += both[:GROUP, :LANES] * both[:GROUP, :LANES] + both[GROUP:, LANES:] * both[GROUP:, LANES:]
        twice[0] += both[:GROUP, LANES:] * both[GROUP:, :LANES]
    return trace[0] + trace[1], once + 2.0 * ((twice[0] + twice[1]) + (twice[2] + twice[3]))


def work_kernel(slab, order, offsets, walk, arrived_ref, rhs_ref, body_ref, old_ref, send_ref, rows_ref, lhs_ref, table_ref):
    blocks = arrived_ref.shape[0]
    occupied, orbitals = body_ref.shape
    rows, _ = packed_rows(occupied)
    folds = send_ref.shape[0] // (blocks * walk)
    wide = folds * LANES
    at_energy, at_exponent, at_old, at_kinetic = offsets
    chunks = [(low, min(low + LANES, orbitals)) for low in range(0, orbitals, LANES)]
    own = lax.axis_index("blk")
    kinetic = jnp.zeros((1, 1), F32)
    force, cross, noise = [], [], []
    lane = lax.broadcasted_iota(jnp.int32, (GROUP, LANES), 1)
    for first in range(0, blocks, GROUP):
        for w in range(GROUP):
            unpack(arrived_ref[order.index(first + w)].astype(F32), rows_ref, w * rows, occupied)
        for j in range(0, occupied, 2):
            for c, (low, high) in enumerate(chunks):
                pair = [rows_ref[c, pl.ds(j + k, GROUP, stride=rows), :] for k in range(2)]
                pair = jnp.concatenate(pair, axis=0).astype(BF16)
                lhs_ref[j * GROUP : (j + 2) * GROUP, low:high] = pair[:, : high - low]
        place = pl.multiple_of(lax.rem(own, GROUP) * rows, TILE)
        here = jnp.zeros((1, 1), F32)
        for c, (low, high) in enumerate(chunks):
            mine = rows_ref[c, pl.ds(place, occupied), :][:, : high - low]
            here += jnp.sum(mine * body_ref[:, low:high], axis=(0, 1), keepdims=True)
        kinetic = jnp.where(own // GROUP == first // GROUP, here, kinetic)
        parts = [rows_ref[0, pl.ds(occupied + k, GROUP, stride=rows), :] for k in range(3)]
        noise.append((parts[0] + parts[1]) + parts[2])
        trace, total = tables_of(lhs_ref[...], rhs_ref, table_ref)
        force.append(jnp.where(lane < slab, trace, 0.0))
        cross.append(jnp.where(lane < slab, total, 0.0))
    force = jnp.concatenate(force, axis=0)
    cross = jnp.concatenate(cross, axis=0)
    noise = jnp.concatenate(noise, axis=0)
    in_slab = lax.broadcasted_iota(jnp.int32, (blocks, LANES), 1) < slab
    shifted = F32(-0.1) * force
    gain = jnp.where(in_slab, noise * shifted + 0.5 * shifted * shifted, 0.0)
    energy = jnp.sum(0.5 * force * force - 0.5 * cross, axis=1, keepdims=True)
    exponent = jnp.sum(gain, axis=1, keepdims=True) - 0.01 * energy
    if wide > LANES:
        force = jnp.concatenate([force, jnp.zeros((blocks, wide - LANES), F32)], axis=1)
    lane = lax.broadcasted_iota(jnp.int32, (blocks, wide), 1)
    row = lax.broadcasted_iota(jnp.int32, (blocks, wide), 0)
    across = jnp.sum(jnp.where(lane - at_exponent == row, exponent, 0.0), axis=0, keepdims=True)
    message = jnp.where(lane < at_energy, force, energy)
    message = jnp.where(lane >= at_exponent, across, message)
    message = jnp.where(lane >= at_old, old_ref[...], message)
    message = jnp.where(lane >= at_kinetic, kinetic, message)
    for k in range(walk * folds):
        c = k % folds
        send_ref[pl.ds(k, blocks, stride=walk * folds), :] = message[:, c * LANES : (c + 1) * LANES]


def finish_kernel(slab, offsets, blocks, walk, got_ref, force_ref, energy_ref, weight_ref, comb_ref):
    folds = got_ref.shape[0] // (blocks * walk)
    wide = folds * LANES
    at_energy, at_exponent, at_old, at_kinetic = offsets
    own_block = lax.axis_index("blk")
    own_walk = lax.axis_index("walk")
    lane = lax.broadcasted_iota(jnp.int32, (blocks, wide), 1)
    row = lax.broadcasted_iota(jnp.int32, (blocks, wide), 0)
    keep = (lane < at_old) | (lane - at_old == row) | (lane - at_kinetic == row)
    own = jnp.zeros((blocks, wide), F32)
    sums = []
    for w in range(walk):
        from_w = [got_ref[pl.ds(w * folds + c, blocks, stride=walk * folds), :] for c in range(folds)]
        from_w = jnp.concatenate(from_w, axis=1)
        own = jnp.where(own_walk == w, from_w, own)
        sums.append(jnp.sum(jnp.where(keep, from_w, 0.0), axis=0, keepdims=True))
    for b in range(blocks):
        force_ref[:, b * slab : (b + 1) * slab] = own[b : b + 1, :slab]
    sums = jnp.concatenate(sums, axis=0)
    exponent = sums[:, at_exponent : at_exponent + blocks]
    old = sums[:, at_old : at_old + blocks]
    kinetic = sums[:, at_kinetic : at_kinetic + blocks]
    weight = old * jnp.exp(exponent - 0.01 * kinetic)
    index = lax.broadcasted_iota(jnp.int32, (walk, blocks), 1) * walk + lax.broadcasted_iota(jnp.int32, (walk, blocks), 0)
    rank = own_block * walk + own_walk

    def total(values):
        return jnp.sum(values, axis=(0, 1), keepdims=True)

    before = total(jnp.where(index < rank, weight, 0.0))
    weight_ref[...] = total(jnp.where(index == rank, weight, 0.0))
    energy_ref[...] = total(jnp.where(lane == at_energy, own, 0.0)) + total(jnp.where(index == rank, kinetic, 0.0))
    comb_ref[...] = before * (blocks * walk) / total(weight) - rank.astype(F32)


def on_device(green_half, chol_half, one_body, field_noise, old_weight):
    slab, occupied, orbitals = chol_half.shape
    blocks = lax.axis_size("blk")
    walk = lax.axis_size("walk")
    order = exchange_order(blocks)
    vmem = pl.BlockSpec(memory_space=pltpu.VMEM)
    hbm = pl.BlockSpec(memory_space=pltpu.HBM)
    first, second = packed_rows(occupied)
    pairs = occupied // 2
    small = pltpu.CompilerParams(vmem_limit_bytes=4 * 2**20)
    message = (blocks, first + second, LANES)
    packed = pl.pallas_call(
        functools.partial(pack_kernel, slab, order),
        out_shape=jax.ShapeDtypeStruct(message, BF16),
        in_specs=[hbm, hbm],
        out_specs=hbm,
        scratch_shapes=[
            pltpu.VMEM(green_half.shape, BF16),
            pltpu.VMEM(field_noise.shape, F32),
            pltpu.VMEM((first, LANES), F32),
            pltpu.VMEM(message, BF16),
            pltpu.SemaphoreType.DMA((2,)),
            pltpu.SemaphoreType.DMA((blocks,)),
        ],
        compiler_params=pltpu.CompilerParams(vmem_limit_bytes=60 * 2**20),
        name="pack",
    )(green_half, field_noise)
    arrived = lax.all_to_all(packed, "blk", split_axis=0, concat_axis=0, axis_index_groups=[order], tiled=True)
    rhs = pl.pallas_call(
        functools.partial(prepare_kernel, slab),
        out_shape=jax.ShapeDtypeStruct((pairs, 2 * LANES, orbitals), BF16),
        in_specs=[vmem],
        out_specs=vmem,
        compiler_params=pltpu.CompilerParams(vmem_limit_bytes=12 * 2**20),
        name="prepare",
    )(jnp.swapaxes(chol_half, 0, 1))
    offsets = (slab, slab + 1, slab + 1 + blocks, slab + 1 + 2 * blocks)
    folds = round_up(slab + 1 + 3 * blocks, LANES) // LANES
    send = pl.pallas_call(
        functools.partial(work_kernel, slab, order, offsets, walk),
        out_shape=jax.ShapeDtypeStruct((blocks * walk * folds, LANES), F32),
        in_specs=[vmem] * 4,
        out_specs=vmem,
        scratch_shapes=[
            pltpu.VMEM((round_up(orbitals, LANES) // LANES, GROUP * first, LANES), F32),
            pltpu.VMEM((GROUP * occupied, orbitals), BF16),
            pltpu.VMEM((pairs, GROUP * occupied, 2 * LANES), F32),
        ],
        compiler_params=pltpu.CompilerParams(vmem_limit_bytes=32 * 2**20),
        name="work",
    )(arrived, rhs, one_body, old_weight.reshape(1, 1))
    got = lax.all_to_all(send, ("blk", "walk"), split_axis=0, concat_axis=0, tiled=True)
    one = jax.ShapeDtypeStruct((1, 1), F32)
    force, energy, weight, comb = pl.pallas_call(
        functools.partial(finish_kernel, slab, offsets, blocks, walk),
        out_shape=(jax.ShapeDtypeStruct((1, slab * blocks), F32), one, one, one),
        in_specs=[vmem],
        out_specs=(vmem,) * 4,
        compiler_params=small,
        name="finish",
    )(got)
    return force, energy.reshape(1), weight.reshape(1), comb.reshape(1)


def solution(mesh):
    placed = (
        P(("blk", "walk"), None, None),
        P("blk", None, None),
        P(),
        P(("blk", "walk"), None),
        P(("blk", "walk")),
    )
    return jax.shard_map(
        on_device,
        mesh=mesh,
        in_specs=placed,
        out_specs=(
            P(("blk", "walk"), None),
            P(("blk", "walk")),
            P(("blk", "walk")),
            P(("blk", "walk")),
        ),
        check_vma=False,
    )
```

```python
import functools

import jax
import jax.numpy as jnp
from jax import lax
from jax.experimental import pallas as pl
from jax.experimental.pallas import tpu as pltpu
from jax.sharding import PartitionSpec as P

F32 = jnp.float32
BF16 = jnp.bfloat16
LANES = 128
TILE = 8
HALF = LANES // 2
GROUP = 8


def round_up(value, unit):
    return -(-value // unit) * unit


def split_three(values):
    high = values.astype(BF16)
    rest = values - high.astype(F32)
    middle = rest.astype(BF16)
    low = (rest - middle.astype(F32)).astype(BF16)
    return high, middle, low


def exchange_order(blocks):
    if blocks % 4:
        return list(range(blocks))
    half = blocks // 4
    return [2 * z + x for low in range(half - 1, -1, -1) for x in (1, 0) for z in (low, low + half)]


MESSAGE = 80
STRIDE = 56
SIDE = 48


def tile_iotas():
    shape = (TILE, LANES)
    return lax.broadcasted_iota(jnp.int32, shape, 0), lax.broadcasted_iota(jnp.int32, shape, 1)


def turned(tile, lanes=0, rows=0):
    tile = pltpu.roll(tile, lanes % LANES, 1) if lanes % LANES else tile
    return pltpu.roll(tile, rows % TILE, 0) if rows % TILE else tile


def pack_kernel(slab, order, green_hbm, noise_hbm, packed_hbm, green_ref, noise_ref, wide_ref, packed_ref, in_sems, out_sems):
    occupied, orbitals = green_ref.shape[1:]
    copies = [
        pltpu.make_async_copy(green_hbm, green_ref, in_sems.at[0]),
        pltpu.make_async_copy(noise_hbm, noise_ref, in_sems.at[1]),
    ]
    for copy in copies:
        copy.start()
    wide_ref[...] = jnp.zeros_like(wide_ref)
    for copy in copies:
        copy.wait()
    wide_ref[0, :occupied, :] = green_ref[0, :, :LANES].astype(F32)
    wide_ref[1, :occupied, : orbitals - LANES] = green_ref[0, :, LANES:].astype(F32)
    rest = [wide_ref[1, t * TILE : (t + 1) * TILE, :] for t in range(STRIDE // TILE)]
    row, lane = tile_iotas()
    folded = [jnp.where(lane < HALF, rest[t], turned(rest[t + 3], HALF)) for t in range(3)]
    last, after = wide_ref[0, SIDE:STRIDE, :], rest[6]
    side = turned(last, SIDE)
    side = jnp.where((row == 2) | (row == 3), jnp.where(lane < 96, turned(last, -32, 2), turned(after, 56, 2)), side)
    side = jnp.where(row == 4, jnp.where(lane < 88, turned(after, SIDE, 4), turned(after, 88, 3)), side)
    for t in range(6):
        side = jnp.where((lane >= t * TILE) & (lane < (t + 1) * TILE), turned(rest[t], t * TILE - HALF), side)
    whole = wide_ref[0, :SIDE, :]
    noise = noise_ref[...]
    sends = []
    for slot, block in enumerate(order):
        piece = noise[:, block * slab : (block + 1) * slab]
        piece = jnp.concatenate([jnp.zeros((1, SIDE), F32), piece, jnp.zeros((1, LANES - SIDE - slab), F32)], axis=1)
        final = side
        for k, part in enumerate(split_three(piece)):
            final = jnp.where((row == 5 + k) & (lane >= SIDE), part.astype(F32), final)
        packed_ref[slot] = jnp.concatenate([whole, *folded, final], axis=0).astype(BF16)
        sends.append(pltpu.make_async_copy(packed_ref.at[slot], packed_hbm.at[slot], out_sems.at[slot]))
        sends[-1].start()
    for send in sends:
        send.wait()


def unpack(packed, rows_ref, at):
    row, lane = tile_iotas()
    side = packed[MESSAGE - TILE :]
    rows_ref[0, at : at + SIDE, :] = packed[:SIDE]
    for t in range(6):
        place = SIDE + (t % 3) * TILE
        tile = turned(packed[place : place + TILE], HALF if t >= 3 else 0)
        rows_ref[1, at + t * TILE : at + (t + 1) * TILE, :] = jnp.where(lane < HALF, tile, turned(side, HALF - t * TILE))
    first = turned(side, -SIDE)
    rows_ref[0, at + SIDE : at + STRIDE, :] = jnp.where((row >= 5) | (lane < 80), first, turned(side, 32, -2))
    tail = jnp.where(row == 0, turned(first, 0, -4), turned(side, -88, -3))
    rows_ref[1, at + SIDE : at + STRIDE, :] = jnp.where(lane < 40, tail, turned(side, -56, -2))


def prepare_kernel(slab, chol_ref, rhs_ref):
    for i in range(chol_ref.shape[0]):
        rhs_ref[i // 2, (i % 2) * LANES : (i % 2) * LANES + slab, :] = chol_ref[i]


def tables_of(lhs, rhs_ref, table_ref):
    trace = [jnp.zeros((GROUP, LANES), F32) for _ in range(2)]
    twice = [jnp.zeros((GROUP, LANES), F32) for _ in range(4)]
    once = jnp.zeros((GROUP, LANES), F32)
    for p in range(rhs_ref.shape[0]):
        table_ref[p] = lax.dot_general(lhs, rhs_ref[p], (((1,), (1,)), ((), ())), preferred_element_type=F32)
        for q in range(p):
            mine = table_ref[p, q * 2 * GROUP : (q + 1) * 2 * GROUP, :]
            other = table_ref[q, p * 2 * GROUP : (p + 1) * 2 * GROUP, :]
            twice[0] += mine[:GROUP, :LANES] * other[:GROUP, :LANES]
            twice[1] += mine[:GROUP, LANES:] * other[GROUP:, :LANES]
            twice[2] += mine[GROUP:, :LANES] * other[:GROUP, LANES:]
            twice[3] += mine[GROUP:, LANES:] * other[GROUP:, LANES:]
        both = table_ref[p, p * 2 * GROUP : (p + 1) * 2 * GROUP, :]
        trace[0] += both[:GROUP, :LANES]
        trace[1] += both[GROUP:, LANES:]
        once += both[:GROUP, :LANES] * both[:GROUP, :LANES] + both[GROUP:, LANES:] * both[GROUP:, LANES:]
        twice[0] += both[:GROUP, LANES:] * both[GROUP:, :LANES]
    return trace[0] + trace[1], once + 2.0 * ((twice[0] + twice[1]) + (twice[2] + twice[3]))


def work_kernel(slab, order, offsets, walk, arrived_ref, rhs_ref, body_ref, old_ref, send_ref, rows_ref, lhs_ref, table_ref):
    blocks = arrived_ref.shape[0]
    occupied, orbitals = body_ref.shape
    rows = STRIDE
    folds = send_ref.shape[0] // (blocks * walk)
    wide = folds * LANES
    at_energy, at_exponent, at_old, at_kinetic = offsets
    chunks = [(low, min(low + LANES, orbitals)) for low in range(0, orbitals, LANES)]
    own = lax.axis_index("blk")
    kinetic = jnp.zeros((1, 1), F32)
    force, cross, noise = [], [], []
    lane = lax.broadcasted_iota(jnp.int32, (GROUP, LANES), 1)
    for first in range(0, blocks, GROUP):
        for w in range(GROUP):
            unpack(arrived_ref[order.index(first + w)].astype(F32), rows_ref, w * rows)
        for j in range(0, occupied, 2):
            for c, (low, high) in enumerate(chunks):
                pair = [rows_ref[c, pl.ds(j + k, GROUP, stride=rows), :] for k in range(2)]
                pair = jnp.concatenate(pair, axis=0).astype(BF16)
                lhs_ref[j * GROUP : (j + 2) * GROUP, low:high] = pair[:, : high - low]
        place = pl.multiple_of(lax.rem(own, GROUP) * rows, TILE)
        here = jnp.zeros((1, 1), F32)
        for c, (low, high) in enumerate(chunks):
            mine = rows_ref[c, pl.ds(place, occupied), :][:, : high - low]
            here += jnp.sum(mine * body_ref[:, low:high], axis=(0, 1), keepdims=True)
        kinetic = jnp.where(own // GROUP == first // GROUP, here, kinetic)
        parts = [rows_ref[0, pl.ds(rows - 3 + k, GROUP, stride=rows), :] for k in range(3)]
        noise.append((parts[0] + parts[1]) + parts[2])
        trace, total = tables_of(lhs_ref[...], rhs_ref, table_ref)
        force.append(jnp.where(lane < slab, trace, 0.0))
        cross.append(jnp.where(lane < slab, total, 0.0))
    force = jnp.concatenate(force, axis=0)
    cross = jnp.concatenate(cross, axis=0)
    noise = jnp.concatenate(noise, axis=0)
    in_slab = lax.broadcasted_iota(jnp.int32, (blocks, LANES), 1) < slab
    shifted = F32(-0.1) * force
    gain = jnp.where(in_slab, noise * shifted + 0.5 * shifted * shifted, 0.0)
    energy = jnp.sum(0.5 * force * force - 0.5 * cross, axis=1, keepdims=True)
    exponent = jnp.sum(gain, axis=1, keepdims=True) - 0.01 * energy
    if wide > LANES:
        force = jnp.concatenate([force, jnp.zeros((blocks, wide - LANES), F32)], axis=1)
    lane = lax.broadcasted_iota(jnp.int32, (blocks, wide), 1)
    row = lax.broadcasted_iota(jnp.int32, (blocks, wide), 0)
    across = jnp.sum(jnp.where(lane - at_exponent == row, exponent, 0.0), axis=0, keepdims=True)
    message = jnp.where(lane < at_energy, force, energy)
    message = jnp.where(lane >= at_exponent, across, message)
    message = jnp.where(lane >= at_old, old_ref[...], message)
    message = jnp.where(lane >= at_kinetic, kinetic, message)
    for k in range(walk * folds):
        c = k % folds
        send_ref[pl.ds(k, blocks, stride=walk * folds), :] = message[:, c * LANES : (c + 1) * LANES]


def finish_kernel(slab, offsets, blocks, walk, got_ref, force_ref, energy_ref, weight_ref, comb_ref):
    folds = got_ref.shape[0] // (blocks * walk)
    wide = folds * LANES
    at_energy, at_exponent, at_old, at_kinetic = offsets
    own_block = lax.axis_index("blk")
    own_walk = lax.axis_index("walk")
    lane = lax.broadcasted_iota(jnp.int32, (blocks, wide), 1)
    row = lax.broadcasted_iota(jnp.int32, (blocks, wide), 0)
    keep = (lane < at_old) | (lane - at_old == row) | (lane - at_kinetic == row)
    own = jnp.zeros((blocks, wide), F32)
    sums = []
    for w in range(walk):
        from_w = [got_ref[pl.ds(w * folds + c, blocks, stride=walk * folds), :] for c in range(folds)]
        from_w = jnp.concatenate(from_w, axis=1)
        own = jnp.where(own_walk == w, from_w, own)
        sums.append(jnp.sum(jnp.where(keep, from_w, 0.0), axis=0, keepdims=True))
    for b in range(blocks):
        force_ref[:, b * slab : (b + 1) * slab] = own[b : b + 1, :slab]
    sums = jnp.concatenate(sums, axis=0)
    exponent = sums[:, at_exponent : at_exponent + blocks]
    old = sums[:, at_old : at_old + blocks]
    kinetic = sums[:, at_kinetic : at_kinetic + blocks]
    weight = old * jnp.exp(exponent - 0.01 * kinetic)
    index = lax.broadcasted_iota(jnp.int32, (walk, blocks), 1) * walk + lax.broadcasted_iota(jnp.int32, (walk, blocks), 0)
    rank = own_block * walk + own_walk

    def total(values):
        return jnp.sum(values, axis=(0, 1), keepdims=True)

    before = total(jnp.where(index < rank, weight, 0.0))
    weight_ref[...] = total(jnp.where(index == rank, weight, 0.0))
    energy_ref[...] = total(jnp.where(lane == at_energy, own, 0.0)) + total(jnp.where(index == rank, kinetic, 0.0))
    comb_ref[...] = before * (blocks * walk) / total(weight) - rank.astype(F32)


def on_device(green_half, chol_half, one_body, field_noise, old_weight):
    slab, occupied, orbitals = chol_half.shape
    blocks = lax.axis_size("blk")
    walk = lax.axis_size("walk")
    order = exchange_order(blocks)
    vmem = pl.BlockSpec(memory_space=pltpu.VMEM)
    hbm = pl.BlockSpec(memory_space=pltpu.HBM)
    pairs = occupied // 2
    small = pltpu.CompilerParams(vmem_limit_bytes=4 * 2**20)
    message = (blocks, MESSAGE, LANES)
    packed = pl.pallas_call(
        functools.partial(pack_kernel, slab, order),
        out_shape=jax.ShapeDtypeStruct(message, BF16),
        in_specs=[hbm, hbm],
        out_specs=hbm,
        scratch_shapes=[
            pltpu.VMEM(green_half.shape, BF16),
            pltpu.VMEM(field_noise.shape, F32),
            pltpu.VMEM((2, STRIDE, LANES), F32),
            pltpu.VMEM(message, BF16),
            pltpu.SemaphoreType.DMA((2,)),
            pltpu.SemaphoreType.DMA((blocks,)),
        ],
        compiler_params=pltpu.CompilerParams(vmem_limit_bytes=60 * 2**20),
        name="pack",
    )(green_half, field_noise)
    arrived = lax.all_to_all(packed, "blk", split_axis=0, concat_axis=0, axis_index_groups=[order], tiled=True)
    rhs = pl.pallas_call(
        functools.partial(prepare_kernel, slab),
        out_shape=jax.ShapeDtypeStruct((pairs, 2 * LANES, orbitals), BF16),
        in_specs=[vmem],
        out_specs=vmem,
        compiler_params=pltpu.CompilerParams(vmem_limit_bytes=12 * 2**20),
        name="prepare",
    )(jnp.swapaxes(chol_half, 0, 1))
    offsets = (slab, slab + 1, slab + 1 + blocks, slab + 1 + 2 * blocks)
    folds = round_up(slab + 1 + 3 * blocks, LANES) // LANES
    send = pl.pallas_call(
        functools.partial(work_kernel, slab, order, offsets, walk),
        out_shape=jax.ShapeDtypeStruct((blocks * walk * folds, LANES), F32),
        in_specs=[vmem] * 4,
        out_specs=vmem,
        scratch_shapes=[
            pltpu.VMEM((round_up(orbitals, LANES) // LANES, GROUP * STRIDE, LANES), F32),
            pltpu.VMEM((GROUP * occupied, orbitals), BF16),
            pltpu.VMEM((pairs, GROUP * occupied, 2 * LANES), F32),
        ],
        compiler_params=pltpu.CompilerParams(vmem_limit_bytes=32 * 2**20),
        name="work",
    )(arrived, rhs, one_body, old_weight.reshape(1, 1))
    got = lax.all_to_all(send, ("blk", "walk"), split_axis=0, concat_axis=0, tiled=True)
    one = jax.ShapeDtypeStruct((1, 1), F32)
    force, energy, weight, comb = pl.pallas_call(
        functools.partial(finish_kernel, slab, offsets, blocks, walk),
        out_shape=(jax.ShapeDtypeStruct((1, slab * blocks), F32), one, one, one),
        in_specs=[vmem],
        out_specs=(vmem,) * 4,
        compiler_params=small,
        name="finish",
    )(got)
    return force, energy.reshape(1), weight.reshape(1), comb.reshape(1)


def solution(mesh):
    placed = (
        P(("blk", "walk"), None, None),
        P("blk", None, None),
        P(),
        P(("blk", "walk"), None),
        P(("blk", "walk")),
    )
    return jax.shard_map(
        on_device,
        mesh=mesh,
        in_specs=placed,
        out_specs=(
            P(("blk", "walk"), None),
            P(("blk", "walk")),
            P(("blk", "walk")),
            P(("blk", "walk")),
        ),
        check_vma=False,
    )
```

```python
import functools

import jax
import jax.numpy as jnp
from jax import lax
from jax.experimental import pallas as pl
from jax.experimental.pallas import tpu as pltpu
from jax.sharding import PartitionSpec as P

F32 = jnp.float32
BF16 = jnp.bfloat16
LANES = 128
TILE = 8
HALF = LANES // 2
SLOT = LANES // TILE
GROUP = 8


def round_up(value, unit):
    return -(-value // unit) * unit


def split_three(values):
    high = values.astype(BF16)
    rest = values - high.astype(F32)
    middle = rest.astype(BF16)
    low = (rest - middle.astype(F32)).astype(BF16)
    return high, middle, low


def exchange_order(blocks):
    if blocks % 4:
        return list(range(blocks))
    half = blocks // 4
    return [2 * z + x for low in range(half - 1, -1, -1) for x in (1, 0) for z in (low, low + half)]


MESSAGE = 80
STRIDE = 56
SIDE = 48


def tile_iotas():
    shape = (TILE, LANES)
    return lax.broadcasted_iota(jnp.int32, shape, 0), lax.broadcasted_iota(jnp.int32, shape, 1)


def turned(tile, lanes=0, rows=0):
    tile = pltpu.roll(tile, lanes % LANES, 1) if lanes % LANES else tile
    return pltpu.roll(tile, rows % TILE, 0) if rows % TILE else tile


def pack_kernel(slab, order, green_hbm, noise_hbm, packed_hbm, green_ref, noise_ref, wide_ref, packed_ref, in_sems, out_sems):
    occupied, orbitals = green_ref.shape[1:]
    copies = [
        pltpu.make_async_copy(green_hbm, green_ref, in_sems.at[0]),
        pltpu.make_async_copy(noise_hbm, noise_ref, in_sems.at[1]),
    ]
    for copy in copies:
        copy.start()
    wide_ref[...] = jnp.zeros_like(wide_ref)
    for copy in copies:
        copy.wait()
    wide_ref[0, :occupied, :] = green_ref[0, :, :LANES].astype(F32)
    wide_ref[1, :occupied, : orbitals - LANES] = green_ref[0, :, LANES:].astype(F32)
    rest = [wide_ref[1, t * TILE : (t + 1) * TILE, :] for t in range(STRIDE // TILE)]
    row, lane = tile_iotas()
    folded = [jnp.where(lane < HALF, rest[t], turned(rest[t + 3], HALF)) for t in range(3)]
    last, after = wide_ref[0, SIDE:STRIDE, :], rest[6]
    side = turned(last, SIDE)
    side = jnp.where((row == 2) | (row == 3), jnp.where(lane < 96, turned(last, -32, 2), turned(after, 56, 2)), side)
    side = jnp.where(row == 4, jnp.where(lane < 88, turned(after, SIDE, 4), turned(after, 88, 3)), side)
    for t in range(6):
        side = jnp.where((lane >= t * TILE) & (lane < (t + 1) * TILE), turned(rest[t], t * TILE - HALF), side)
    whole = wide_ref[0, :SIDE, :]
    noise = noise_ref[...]
    sends = []
    for slot, block in enumerate(order):
        piece = noise[:, block * slab : (block + 1) * slab]
        piece = jnp.concatenate([jnp.zeros((1, SIDE), F32), piece, jnp.zeros((1, LANES - SIDE - slab), F32)], axis=1)
        final = side
        for k, part in enumerate(split_three(piece)):
            final = jnp.where((row == 5 + k) & (lane >= SIDE), part.astype(F32), final)
        packed_ref[slot] = jnp.concatenate([whole, *folded, final], axis=0).astype(BF16)
        sends.append(pltpu.make_async_copy(packed_ref.at[slot], packed_hbm.at[slot], out_sems.at[slot]))
        sends[-1].start()
    for send in sends:
        send.wait()


def unpack(packed, rows_ref, at):
    row, lane = tile_iotas()
    side = packed[MESSAGE - TILE :]
    rows_ref[0, at : at + SIDE, :] = packed[:SIDE]
    for t in range(6):
        place = SIDE + (t % 3) * TILE
        tile = turned(packed[place : place + TILE], HALF if t >= 3 else 0)
        rows_ref[1, at + t * TILE : at + (t + 1) * TILE, :] = jnp.where(lane < HALF, tile, turned(side, HALF - t * TILE))
    first = turned(side, -SIDE)
    rows_ref[0, at + SIDE : at + STRIDE, :] = jnp.where((row >= 5) | (lane < 80), first, turned(side, 32, -2))
    tail = jnp.where(row == 0, turned(first, 0, -4), turned(side, -88, -3))
    rows_ref[1, at + SIDE : at + STRIDE, :] = jnp.where(lane < 40, tail, turned(side, -56, -2))


def plan_of(occupied):
    tiles = [("pair", p) for p in range(-(-occupied // 2))]
    tiles += [("eight", e) for e in range(-(-occupied // TILE))]
    tiles = tiles[::-1]
    place = {tile: divmod(k, 2) for k, tile in enumerate(tiles)}
    pairs = [place["pair", p] for p in range(-(-occupied // 2))]
    eights = [place["eight", e] for e in range(-(-occupied // TILE))]
    return pairs, eights, -(-len(tiles) // 2)


def prepare_kernel(slab, chol_ref, rhs_ref):
    occupied = chol_ref.shape[0]
    pairs, eights, products = plan_of(occupied)
    for p, t in eights + [(products - 1, 1)]:
        rhs_ref[p, t * LANES : (t + 1) * LANES, :] = jnp.zeros((LANES, rhs_ref.shape[2]), BF16)
    for i in range(occupied):
        p, t = pairs[i // 2]
        start = t * LANES + i % 2 * HALF
        rhs_ref[p, start : start + HALF, :] = chol_ref[i, :HALF, :]
        p, t = eights[i // TILE]
        start = t * LANES + i % TILE * SLOT
        rhs_ref[p, start : start + slab - HALF, :] = chol_ref[i, HALF:, :]


def tables_of(lhs, rhs_ref, table_ref):
    occupied = lhs.shape[0] // GROUP
    pairs, eights, products = plan_of(occupied)
    _, lane = tile_iotas()
    low = lane < HALF
    zero = jnp.zeros((GROUP, LANES), F32)
    at = {place: ("pair", k) for k, place in enumerate(pairs)} | {place: ("eight", k) for k, place in enumerate(eights)}

    def tile(place, j):
        if j >= occupied:
            return zero
        p, t = place
        return table_ref[p, j * GROUP : (j + 1) * GROUP, t * LANES : (t + 1) * LANES]

    def diagonals(tiles):
        for d in (1, 2, 4):
            keep = (lane // SLOT) & d == 0
            tiles = [jnp.where(keep, tiles[r], tiles[(r + d) % TILE]) for r in range(TILE)]
        return tiles

    def products_of(mine, other):
        return [mine[r] * turned(other[-r % TILE], -r * SLOT) for r in range(TILE)]

    once, twice = [zero] * 2, [zero] * 4
    trace, ends = [zero] * 2, zero
    done = {"pair": [], "eight": []}
    for p in range(products):
        table_ref[p] = lax.dot_general(lhs, rhs_ref[p], (((1,), (1,)), ((), ())), preferred_element_type=F32)
        for t in range(2):
            kind, k = at.get((p, t), (None, 0))
            if kind == "pair":
                for q in done[kind]:
                    mine = [tile(pairs[k], 2 * q), tile(pairs[k], 2 * q + 1)]
                    other = [tile(pairs[q], 2 * k), tile(pairs[q], 2 * k + 1)]
                    twice[0] += jnp.where(low, mine[0], mine[1]) * jnp.where(low, other[0], other[1])
                    twice[1] += jnp.where(low, mine[1], mine[0]) * turned(jnp.where(low, other[1], other[0]), HALF)
                mine = [tile(pairs[k], 2 * k), tile(pairs[k], 2 * k + 1)]
                both = jnp.where(low, mine[0], mine[1])
                trace[k % 2] += both
                once[0] += both * both
                twice[2] += jnp.where(low, turned(mine[0], HALF) * mine[1], 0.0)
                done[kind].append(k)
            elif kind == "eight":
                mine = diagonals([tile(eights[k], TILE * k + j) for j in range(TILE)])
                ends += mine[0]
                for product in products_of(mine, mine):
                    once[1] += product
                for q in done[kind]:
                    mine = diagonals([tile(eights[k], TILE * q + j) for j in range(TILE)])
                    other = diagonals([tile(eights[q], TILE * k + j) for j in range(TILE)])
                    for product in products_of(mine, other):
                        twice[3] += product
                done[kind].append(k)
    trace = trace[0] + trace[1]
    trace = trace + turned(trace, HALF)
    for lanes in (HALF, HALF // 2, HALF // 4):
        ends = ends + turned(ends, lanes)
    total = once[0] + once[1] + 2.0 * ((twice[0] + twice[1]) + (twice[2] + twice[3]))
    return jnp.where(low, trace, ends), total


def work_kernel(slab, order, offsets, walk, arrived_ref, rhs_ref, body_ref, old_ref, send_ref, rows_ref, lhs_ref, table_ref):
    blocks = arrived_ref.shape[0]
    occupied, orbitals = body_ref.shape
    rows = STRIDE
    folds = send_ref.shape[0] // (blocks * walk)
    wide = folds * LANES
    at_energy, at_exponent, at_old, at_kinetic = offsets
    chunks = [(low, min(low + LANES, orbitals)) for low in range(0, orbitals, LANES)]
    own = lax.axis_index("blk")
    kinetic = jnp.zeros((1, 1), F32)
    force, cross, noise = [], [], []
    lane = lax.broadcasted_iota(jnp.int32, (GROUP, LANES), 1)
    for first in range(0, blocks, GROUP):
        for w in range(GROUP):
            unpack(arrived_ref[order.index(first + w)].astype(F32), rows_ref, w * rows)
        for j in range(0, occupied, 2):
            for c, (low, high) in enumerate(chunks):
                pair = [rows_ref[c, pl.ds(j + k, GROUP, stride=rows), :] for k in range(2)]
                pair = jnp.concatenate(pair, axis=0).astype(BF16)
                lhs_ref[j * GROUP : (j + 2) * GROUP, low:high] = pair[:, : high - low]
        place = pl.multiple_of(lax.rem(own, GROUP) * rows, TILE)
        here = jnp.zeros((1, 1), F32)
        for c, (low, high) in enumerate(chunks):
            mine = rows_ref[c, pl.ds(place, occupied), :][:, : high - low]
            here += jnp.sum(mine * body_ref[:, low:high], axis=(0, 1), keepdims=True)
        kinetic = jnp.where(own // GROUP == first // GROUP, here, kinetic)
        parts = [rows_ref[0, pl.ds(rows - 3 + k, GROUP, stride=rows), :] for k in range(3)]
        noise.append((parts[0] + parts[1]) + parts[2])
        trace, total = tables_of(lhs_ref[...], rhs_ref, table_ref)
        force.append(jnp.where(lane < slab, trace, 0.0))
        cross.append(total)
    force = jnp.concatenate(force, axis=0)
    cross = jnp.concatenate(cross, axis=0)
    noise = jnp.concatenate(noise, axis=0)
    in_slab = lax.broadcasted_iota(jnp.int32, (blocks, LANES), 1) < slab
    shifted = F32(-0.1) * force
    gain = jnp.where(in_slab, noise * shifted + 0.5 * shifted * shifted, 0.0)
    energy = jnp.sum(0.5 * force * force - 0.5 * cross, axis=1, keepdims=True)
    exponent = jnp.sum(gain, axis=1, keepdims=True) - 0.01 * energy
    if wide > LANES:
        force = jnp.concatenate([force, jnp.zeros((blocks, wide - LANES), F32)], axis=1)
    lane = lax.broadcasted_iota(jnp.int32, (blocks, wide), 1)
    row = lax.broadcasted_iota(jnp.int32, (blocks, wide), 0)
    across = jnp.sum(jnp.where(lane - at_exponent == row, exponent, 0.0), axis=0, keepdims=True)
    message = jnp.where(lane < at_energy, force, energy)
    message = jnp.where(lane >= at_exponent, across, message)
    message = jnp.where(lane >= at_old, old_ref[...], message)
    message = jnp.where(lane >= at_kinetic, kinetic, message)
    for k in range(walk * folds):
        c = k % folds
        send_ref[pl.ds(k, blocks, stride=walk * folds), :] = message[:, c * LANES : (c + 1) * LANES]


def finish_kernel(slab, offsets, blocks, walk, got_ref, force_ref, energy_ref, weight_ref, comb_ref):
    folds = got_ref.shape[0] // (blocks * walk)
    wide = folds * LANES
    at_energy, at_exponent, at_old, at_kinetic = offsets
    own_block = lax.axis_index("blk")
    own_walk = lax.axis_index("walk")
    lane = lax.broadcasted_iota(jnp.int32, (blocks, wide), 1)
    row = lax.broadcasted_iota(jnp.int32, (blocks, wide), 0)
    keep = (lane < at_old) | (lane - at_old == row) | (lane - at_kinetic == row)
    own = jnp.zeros((blocks, wide), F32)
    sums = []
    for w in range(walk):
        from_w = [got_ref[pl.ds(w * folds + c, blocks, stride=walk * folds), :] for c in range(folds)]
        from_w = jnp.concatenate(from_w, axis=1)
        own = jnp.where(own_walk == w, from_w, own)
        sums.append(jnp.sum(jnp.where(keep, from_w, 0.0), axis=0, keepdims=True))
    for b in range(blocks):
        force_ref[:, b * slab : (b + 1) * slab] = own[b : b + 1, :slab]
    sums = jnp.concatenate(sums, axis=0)
    exponent = sums[:, at_exponent : at_exponent + blocks]
    old = sums[:, at_old : at_old + blocks]
    kinetic = sums[:, at_kinetic : at_kinetic + blocks]
    weight = old * jnp.exp(exponent - 0.01 * kinetic)
    index = lax.broadcasted_iota(jnp.int32, (walk, blocks), 1) * walk + lax.broadcasted_iota(jnp.int32, (walk, blocks), 0)
    rank = own_block * walk + own_walk

    def total(values):
        return jnp.sum(values, axis=(0, 1), keepdims=True)

    before = total(jnp.where(index < rank, weight, 0.0))
    weight_ref[...] = total(jnp.where(index == rank, weight, 0.0))
    energy_ref[...] = total(jnp.where(lane == at_energy, own, 0.0)) + total(jnp.where(index == rank, kinetic, 0.0))
    comb_ref[...] = before * (blocks * walk) / total(weight) - rank.astype(F32)


def on_device(green_half, chol_half, one_body, field_noise, old_weight):
    slab, occupied, orbitals = chol_half.shape
    blocks = lax.axis_size("blk")
    walk = lax.axis_size("walk")
    order = exchange_order(blocks)
    vmem = pl.BlockSpec(memory_space=pltpu.VMEM)
    hbm = pl.BlockSpec(memory_space=pltpu.HBM)
    products = plan_of(occupied)[2]
    small = pltpu.CompilerParams(vmem_limit_bytes=4 * 2**20)
    message = (blocks, MESSAGE, LANES)
    packed = pl.pallas_call(
        functools.partial(pack_kernel, slab, order),
        out_shape=jax.ShapeDtypeStruct(message, BF16),
        in_specs=[hbm, hbm],
        out_specs=hbm,
        scratch_shapes=[
            pltpu.VMEM(green_half.shape, BF16),
            pltpu.VMEM(field_noise.shape, F32),
            pltpu.VMEM((2, STRIDE, LANES), F32),
            pltpu.VMEM(message, BF16),
            pltpu.SemaphoreType.DMA((2,)),
            pltpu.SemaphoreType.DMA((blocks,)),
        ],
        compiler_params=pltpu.CompilerParams(vmem_limit_bytes=60 * 2**20),
        name="pack",
    )(green_half, field_noise)
    arrived = lax.all_to_all(packed, "blk", split_axis=0, concat_axis=0, axis_index_groups=[order], tiled=True)
    rhs = pl.pallas_call(
        functools.partial(prepare_kernel, slab),
        out_shape=jax.ShapeDtypeStruct((products, 2 * LANES, orbitals), BF16),
        in_specs=[vmem],
        out_specs=vmem,
        compiler_params=pltpu.CompilerParams(vmem_limit_bytes=12 * 2**20),
        name="prepare",
    )(jnp.swapaxes(chol_half, 0, 1))
    offsets = (slab, slab + 1, slab + 1 + blocks, slab + 1 + 2 * blocks)
    folds = round_up(slab + 1 + 3 * blocks, LANES) // LANES
    send = pl.pallas_call(
        functools.partial(work_kernel, slab, order, offsets, walk),
        out_shape=jax.ShapeDtypeStruct((blocks * walk * folds, LANES), F32),
        in_specs=[vmem] * 4,
        out_specs=vmem,
        scratch_shapes=[
            pltpu.VMEM((round_up(orbitals, LANES) // LANES, GROUP * STRIDE, LANES), F32),
            pltpu.VMEM((GROUP * occupied, orbitals), BF16),
            pltpu.VMEM((products, GROUP * occupied, 2 * LANES), F32),
        ],
        compiler_params=pltpu.CompilerParams(vmem_limit_bytes=32 * 2**20),
        name="work",
    )(arrived, rhs, one_body, old_weight.reshape(1, 1))
    got = lax.all_to_all(send, ("blk", "walk"), split_axis=0, concat_axis=0, tiled=True)
    one = jax.ShapeDtypeStruct((1, 1), F32)
    force, energy, weight, comb = pl.pallas_call(
        functools.partial(finish_kernel, slab, offsets, blocks, walk),
        out_shape=(jax.ShapeDtypeStruct((1, slab * blocks), F32), one, one, one),
        in_specs=[vmem],
        out_specs=(vmem,) * 4,
        compiler_params=small,
        name="finish",
    )(got)
    return force, energy.reshape(1), weight.reshape(1), comb.reshape(1)


def solution(mesh):
    placed = (
        P(("blk", "walk"), None, None),
        P("blk", None, None),
        P(),
        P(("blk", "walk"), None),
        P(("blk", "walk")),
    )
    return jax.shard_map(
        on_device,
        mesh=mesh,
        in_specs=placed,
        out_specs=(
            P(("blk", "walk"), None),
            P(("blk", "walk")),
            P(("blk", "walk")),
            P(("blk", "walk")),
        ),
        check_vma=False,
    )
```

```python
import functools

import jax
import jax.numpy as jnp
from jax import lax
from jax.experimental import pallas as pl
from jax.experimental.pallas import tpu as pltpu
from jax.sharding import PartitionSpec as P

F32 = jnp.float32
BF16 = jnp.bfloat16
LANES = 128
TILE = 8
HALF = LANES // 2
SLOT = LANES // TILE
GROUP = 8


def round_up(value, unit):
    return -(-value // unit) * unit


def split_three(values):
    high = values.astype(BF16)
    rest = values - high.astype(F32)
    middle = rest.astype(BF16)
    low = (rest - middle.astype(F32)).astype(BF16)
    return high, middle, low


def exchange_order(blocks):
    if blocks % 2:
        return list(range(blocks))
    half = blocks // 2
    return [block for low in [half - 1, *range(half - 1)] for block in (low, low + half)]


MESSAGE = 80
STRIDE = 56
SIDE = 48


def tile_iotas():
    shape = (TILE, LANES)
    return lax.broadcasted_iota(jnp.int32, shape, 0), lax.broadcasted_iota(jnp.int32, shape, 1)


def turned(tile, lanes=0, rows=0):
    tile = pltpu.roll(tile, lanes % LANES, 1) if lanes % LANES else tile
    return pltpu.roll(tile, rows % TILE, 0) if rows % TILE else tile


def pack_kernel(slab, order, green_hbm, noise_hbm, packed_hbm, green_ref, noise_ref, wide_ref, packed_ref, in_sems, out_sem):
    occupied, orbitals = green_ref.shape[1:]
    copies = [
        pltpu.make_async_copy(green_hbm, green_ref, in_sems.at[0]),
        pltpu.make_async_copy(noise_hbm, noise_ref, in_sems.at[1]),
    ]
    for copy in copies:
        copy.start()
    wide_ref[...] = jnp.zeros_like(wide_ref)
    for copy in copies:
        copy.wait()
    wide_ref[0, :occupied, :] = green_ref[0, :, :LANES].astype(F32)
    wide_ref[1, :occupied, : orbitals - LANES] = green_ref[0, :, LANES:].astype(F32)
    rest = [wide_ref[1, t * TILE : (t + 1) * TILE, :] for t in range(STRIDE // TILE)]
    row, lane = tile_iotas()
    folded = [jnp.where(lane < HALF, rest[t], turned(rest[t + 3], HALF)) for t in range(3)]
    last, after = wide_ref[0, SIDE:STRIDE, :], rest[6]
    side = turned(last, SIDE)
    side = jnp.where((row == 2) | (row == 3), jnp.where(lane < 96, turned(last, -32, 2), turned(after, 56, 2)), side)
    side = jnp.where(row == 4, jnp.where(lane < 88, turned(after, SIDE, 4), turned(after, 88, 3)), side)
    for t in range(6):
        side = jnp.where((lane >= t * TILE) & (lane < (t + 1) * TILE), turned(rest[t], t * TILE - HALF), side)
    whole = wide_ref[0, :SIDE, :]
    noise = noise_ref[...]
    for slot, block in enumerate(order):
        piece = noise[:, block * slab : (block + 1) * slab]
        piece = jnp.concatenate([jnp.zeros((1, SIDE), F32), piece, jnp.zeros((1, LANES - SIDE - slab), F32)], axis=1)
        final = side
        for k, part in enumerate(split_three(piece)):
            final = jnp.where((row == 5 + k) & (lane >= SIDE), part.astype(F32), final)
        packed_ref[slot] = jnp.concatenate([whole, *folded, final], axis=0).astype(BF16)
    send = pltpu.make_async_copy(packed_ref, packed_hbm, out_sem)
    send.start()
    send.wait()


def unpack(packed, rows_ref, at):
    row, lane = tile_iotas()
    side = packed[MESSAGE - TILE :]
    rows_ref[0, at : at + SIDE, :] = packed[:SIDE]
    for t in range(6):
        place = SIDE + (t % 3) * TILE
        tile = turned(packed[place : place + TILE], HALF if t >= 3 else 0)
        rows_ref[1, at + t * TILE : at + (t + 1) * TILE, :] = jnp.where(lane < HALF, tile, turned(side, HALF - t * TILE))
    first = turned(side, -SIDE)
    rows_ref[0, at + SIDE : at + STRIDE, :] = jnp.where((row >= 5) | (lane < 80), first, turned(side, 32, -2))
    tail = jnp.where(row == 0, turned(first, 0, -4), turned(side, -88, -3))
    rows_ref[1, at + SIDE : at + STRIDE, :] = jnp.where(lane < 40, tail, turned(side, -56, -2))


def plan_of(occupied):
    tiles = [("pair", p) for p in range(-(-occupied // 2))]
    tiles += [("eight", e) for e in range(-(-occupied // TILE))]
    tiles = tiles[::-1]
    place = {tile: divmod(k, 2) for k, tile in enumerate(tiles)}
    pairs = [place["pair", p] for p in range(-(-occupied // 2))]
    eights = [place["eight", e] for e in range(-(-occupied // TILE))]
    return pairs, eights, -(-len(tiles) // 2)


def prepare_kernel(slab, chol_ref, rhs_ref):
    occupied = chol_ref.shape[0]
    pairs, eights, products = plan_of(occupied)
    for p, t in eights + [(products - 1, 1)]:
        rhs_ref[p, t * LANES : (t + 1) * LANES, :] = jnp.zeros((LANES, rhs_ref.shape[2]), BF16)
    for i in range(occupied):
        p, t = pairs[i // 2]
        start = t * LANES + i % 2 * HALF
        rhs_ref[p, start : start + HALF, :] = chol_ref[i, :HALF, :]
        p, t = eights[i // TILE]
        start = t * LANES + i % TILE * SLOT
        rhs_ref[p, start : start + slab - HALF, :] = chol_ref[i, HALF:, :]


def tables_of(lhs, rhs_ref, table_ref):
    occupied = lhs.shape[0] // GROUP
    pairs, eights, products = plan_of(occupied)
    _, lane = tile_iotas()
    low = lane < HALF
    zero = jnp.zeros((GROUP, LANES), F32)
    at = {place: ("pair", k) for k, place in enumerate(pairs)} | {place: ("eight", k) for k, place in enumerate(eights)}

    def tile(place, j):
        if j >= occupied:
            return zero
        p, t = place
        return table_ref[p, j * GROUP : (j + 1) * GROUP, t * LANES : (t + 1) * LANES]

    def diagonals(tiles):
        for d in (1, 2, 4):
            keep = (lane // SLOT) & d == 0
            tiles = [jnp.where(keep, tiles[r], tiles[(r + d) % TILE]) for r in range(TILE)]
        return tiles

    def products_of(mine, other):
        return [mine[r] * turned(other[-r % TILE], -r * SLOT) for r in range(TILE)]

    once, twice = [zero] * 2, [zero] * 4
    trace, ends = [zero] * 2, zero
    done = {"pair": [], "eight": []}
    for p in range(products):
        table_ref[p] = lax.dot_general(lhs, rhs_ref[p], (((1,), (1,)), ((), ())), preferred_element_type=F32)
        for t in range(2):
            kind, k = at.get((p, t), (None, 0))
            if kind == "pair":
                for q in done[kind]:
                    mine = [tile(pairs[k], 2 * q), tile(pairs[k], 2 * q + 1)]
                    other = [tile(pairs[q], 2 * k), tile(pairs[q], 2 * k + 1)]
                    twice[0] += jnp.where(low, mine[0], mine[1]) * jnp.where(low, other[0], other[1])
                    twice[1] += jnp.where(low, mine[1], mine[0]) * turned(jnp.where(low, other[1], other[0]), HALF)
                mine = [tile(pairs[k], 2 * k), tile(pairs[k], 2 * k + 1)]
                both = jnp.where(low, mine[0], mine[1])
                trace[k % 2] += both
                once[0] += both * both
                twice[2] += jnp.where(low, turned(mine[0], HALF) * mine[1], 0.0)
                done[kind].append(k)
            elif kind == "eight":
                mine = diagonals([tile(eights[k], TILE * k + j) for j in range(TILE)])
                ends += mine[0]
                for product in products_of(mine, mine):
                    once[1] += product
                for q in done[kind]:
                    mine = diagonals([tile(eights[k], TILE * q + j) for j in range(TILE)])
                    other = diagonals([tile(eights[q], TILE * k + j) for j in range(TILE)])
                    for product in products_of(mine, other):
                        twice[3] += product
                done[kind].append(k)
    trace = trace[0] + trace[1]
    trace = trace + turned(trace, HALF)
    for lanes in (HALF, HALF // 2, HALF // 4):
        ends = ends + turned(ends, lanes)
    total = once[0] + once[1] + 2.0 * ((twice[0] + twice[1]) + (twice[2] + twice[3]))
    return jnp.where(low, trace, ends), total


def work_kernel(slab, order, offsets, walk, arrived_ref, rhs_ref, body_ref, old_ref, send_ref, rows_ref, lhs_ref, table_ref):
    blocks = arrived_ref.shape[0]
    occupied, orbitals = body_ref.shape
    rows = STRIDE
    folds = send_ref.shape[0] // (blocks * walk)
    wide = folds * LANES
    at_energy, at_exponent, at_old, at_kinetic = offsets
    chunks = [(low, min(low + LANES, orbitals)) for low in range(0, orbitals, LANES)]
    own = lax.axis_index("blk")
    kinetic = jnp.zeros((1, 1), F32)
    force, cross, noise = [], [], []
    lane = lax.broadcasted_iota(jnp.int32, (GROUP, LANES), 1)
    for first in range(0, blocks, GROUP):
        for w in range(GROUP):
            unpack(arrived_ref[order.index(first + w)].astype(F32), rows_ref, w * rows)
        for j in range(0, occupied, 2):
            for c, (low, high) in enumerate(chunks):
                pair = [rows_ref[c, pl.ds(j + k, GROUP, stride=rows), :] for k in range(2)]
                pair = jnp.concatenate(pair, axis=0).astype(BF16)
                lhs_ref[j * GROUP : (j + 2) * GROUP, low:high] = pair[:, : high - low]
        place = pl.multiple_of(lax.rem(own, GROUP) * rows, TILE)
        here = jnp.zeros((1, 1), F32)
        for c, (low, high) in enumerate(chunks):
            mine = rows_ref[c, pl.ds(place, occupied), :][:, : high - low]
            here += jnp.sum(mine * body_ref[:, low:high], axis=(0, 1), keepdims=True)
        kinetic = jnp.where(own // GROUP == first // GROUP, here, kinetic)
        parts = [rows_ref[0, pl.ds(rows - 3 + k, GROUP, stride=rows), :] for k in range(3)]
        noise.append((parts[0] + parts[1]) + parts[2])
        trace, total = tables_of(lhs_ref[...], rhs_ref, table_ref)
        force.append(jnp.where(lane < slab, trace, 0.0))
        cross.append(total)
    force = jnp.concatenate(force, axis=0)
    cross = jnp.concatenate(cross, axis=0)
    noise = jnp.concatenate(noise, axis=0)
    in_slab = lax.broadcasted_iota(jnp.int32, (blocks, LANES), 1) < slab
    shifted = F32(-0.1) * force
    gain = jnp.where(in_slab, noise * shifted + 0.5 * shifted * shifted, 0.0)
    energy = jnp.sum(0.5 * force * force - 0.5 * cross, axis=1, keepdims=True)
    exponent = jnp.sum(gain, axis=1, keepdims=True) - 0.01 * energy
    if wide > LANES:
        force = jnp.concatenate([force, jnp.zeros((blocks, wide - LANES), F32)], axis=1)
    lane = lax.broadcasted_iota(jnp.int32, (blocks, wide), 1)
    row = lax.broadcasted_iota(jnp.int32, (blocks, wide), 0)
    across = jnp.sum(jnp.where(lane - at_exponent == row, exponent, 0.0), axis=0, keepdims=True)
    message = jnp.where(lane < at_energy, force, energy)
    message = jnp.where(lane >= at_exponent, across, message)
    message = jnp.where(lane >= at_old, old_ref[...], message)
    message = jnp.where(lane >= at_kinetic, kinetic, message)
    for k in range(walk * folds):
        c = k % folds
        send_ref[pl.ds(k, blocks, stride=walk * folds), :] = message[:, c * LANES : (c + 1) * LANES]


def finish_kernel(slab, offsets, blocks, walk, got_ref, force_ref, energy_ref, weight_ref, comb_ref):
    folds = got_ref.shape[0] // (blocks * walk)
    wide = folds * LANES
    at_energy, at_exponent, at_old, at_kinetic = offsets
    own_block = lax.axis_index("blk")
    own_walk = lax.axis_index("walk")
    lane = lax.broadcasted_iota(jnp.int32, (blocks, wide), 1)
    row = lax.broadcasted_iota(jnp.int32, (blocks, wide), 0)
    keep = (lane < at_old) | (lane - at_old == row) | (lane - at_kinetic == row)
    own = jnp.zeros((blocks, wide), F32)
    sums = []
    for w in range(walk):
        from_w = [got_ref[pl.ds(w * folds + c, blocks, stride=walk * folds), :] for c in range(folds)]
        from_w = jnp.concatenate(from_w, axis=1)
        own = jnp.where(own_walk == w, from_w, own)
        sums.append(jnp.sum(jnp.where(keep, from_w, 0.0), axis=0, keepdims=True))
    for b in range(blocks):
        force_ref[:, b * slab : (b + 1) * slab] = own[b : b + 1, :slab]
    sums = jnp.concatenate(sums, axis=0)
    exponent = sums[:, at_exponent : at_exponent + blocks]
    old = sums[:, at_old : at_old + blocks]
    kinetic = sums[:, at_kinetic : at_kinetic + blocks]
    weight = old * jnp.exp(exponent - 0.01 * kinetic)
    index = lax.broadcasted_iota(jnp.int32, (walk, blocks), 1) * walk + lax.broadcasted_iota(jnp.int32, (walk, blocks), 0)
    rank = own_block * walk + own_walk

    def total(values):
        return jnp.sum(values, axis=(0, 1), keepdims=True)

    before = total(jnp.where(index < rank, weight, 0.0))
    weight_ref[...] = total(jnp.where(index == rank, weight, 0.0))
    energy_ref[...] = total(jnp.where(lane == at_energy, own, 0.0)) + total(jnp.where(index == rank, kinetic, 0.0))
    comb_ref[...] = before * (blocks * walk) / total(weight) - rank.astype(F32)


def on_device(green_half, chol_half, one_body, field_noise, old_weight):
    slab, occupied, orbitals = chol_half.shape
    blocks = lax.axis_size("blk")
    walk = lax.axis_size("walk")
    order = exchange_order(blocks)
    vmem = pl.BlockSpec(memory_space=pltpu.VMEM)
    hbm = pl.BlockSpec(memory_space=pltpu.HBM)
    products = plan_of(occupied)[2]
    small = pltpu.CompilerParams(vmem_limit_bytes=4 * 2**20)
    message = (blocks, MESSAGE, LANES)
    packed = pl.pallas_call(
        functools.partial(pack_kernel, slab, order),
        out_shape=jax.ShapeDtypeStruct(message, BF16),
        in_specs=[hbm, hbm],
        out_specs=hbm,
        scratch_shapes=[
            pltpu.VMEM(green_half.shape, BF16),
            pltpu.VMEM(field_noise.shape, F32),
            pltpu.VMEM((2, STRIDE, LANES), F32),
            pltpu.VMEM(message, BF16),
            pltpu.SemaphoreType.DMA((2,)),
            pltpu.SemaphoreType.DMA,
        ],
        compiler_params=pltpu.CompilerParams(vmem_limit_bytes=60 * 2**20),
        name="pack",
    )(green_half, field_noise)
    arrived = lax.all_to_all(packed, "blk", split_axis=0, concat_axis=0, axis_index_groups=[order], tiled=True)
    rhs = pl.pallas_call(
        functools.partial(prepare_kernel, slab),
        out_shape=jax.ShapeDtypeStruct((products, 2 * LANES, orbitals), BF16),
        in_specs=[vmem],
        out_specs=vmem,
        compiler_params=pltpu.CompilerParams(vmem_limit_bytes=12 * 2**20),
        name="prepare",
    )(jnp.swapaxes(chol_half, 0, 1))
    offsets = (slab, slab + 1, slab + 1 + blocks, slab + 1 + 2 * blocks)
    folds = round_up(slab + 1 + 3 * blocks, LANES) // LANES
    send = pl.pallas_call(
        functools.partial(work_kernel, slab, order, offsets, walk),
        out_shape=jax.ShapeDtypeStruct((blocks * walk * folds, LANES), F32),
        in_specs=[vmem] * 4,
        out_specs=vmem,
        scratch_shapes=[
            pltpu.VMEM((round_up(orbitals, LANES) // LANES, GROUP * STRIDE, LANES), F32),
            pltpu.VMEM((GROUP * occupied, orbitals), BF16),
            pltpu.VMEM((products, GROUP * occupied, 2 * LANES), F32),
        ],
        compiler_params=pltpu.CompilerParams(vmem_limit_bytes=32 * 2**20),
        name="work",
    )(arrived, rhs, one_body, old_weight.reshape(1, 1))
    got = lax.all_to_all(send, ("blk", "walk"), split_axis=0, concat_axis=0, tiled=True)
    one = jax.ShapeDtypeStruct((1, 1), F32)
    force, energy, weight, comb = pl.pallas_call(
        functools.partial(finish_kernel, slab, offsets, blocks, walk),
        out_shape=(jax.ShapeDtypeStruct((1, slab * blocks), F32), one, one, one),
        in_specs=[vmem],
        out_specs=(vmem,) * 4,
        compiler_params=small,
        name="finish",
    )(got)
    return force, energy.reshape(1), weight.reshape(1), comb.reshape(1)


def solution(mesh):
    placed = (
        P(("blk", "walk"), None, None),
        P("blk", None, None),
        P(),
        P(("blk", "walk"), None),
        P(("blk", "walk")),
    )
    return jax.shard_map(
        on_device,
        mesh=mesh,
        in_specs=placed,
        out_specs=(
            P(("blk", "walk"), None),
            P(("blk", "walk")),
            P(("blk", "walk")),
            P(("blk", "walk")),
        ),
        check_vma=False,
    )
```

```python
import functools

import jax
import jax.numpy as jnp
from jax import lax
from jax.experimental import pallas as pl
from jax.experimental.pallas import tpu as pltpu
from jax.sharding import PartitionSpec as P

F32 = jnp.float32
BF16 = jnp.bfloat16
LANES = 128
TILE = 8
HALF = LANES // 2
SLOT = LANES // TILE
GROUP = 8


def round_up(value, unit):
    return -(-value // unit) * unit


def split_three(values):
    high = values.astype(BF16)
    rest = values - high.astype(F32)
    middle = rest.astype(BF16)
    low = (rest - middle.astype(F32)).astype(BF16)
    return high, middle, low


def exchange_order(blocks):
    if blocks % 2:
        return list(range(blocks))
    half = blocks // 2
    return [block for low in [half - 1, *range(half - 1)] for block in (low, low + half)]


MESSAGE = 80
STRIDE = 56
SIDE = 48


def tile_iotas():
    shape = (TILE, LANES)
    return lax.broadcasted_iota(jnp.int32, shape, 0), lax.broadcasted_iota(jnp.int32, shape, 1)


def turned(tile, lanes=0, rows=0):
    tile = pltpu.roll(tile, lanes % LANES, 1) if lanes % LANES else tile
    return pltpu.roll(tile, rows % TILE, 0) if rows % TILE else tile


def pack_kernel(slab, order, green_ref, noise_ref, packed_ref, wide_ref):
    occupied, orbitals = green_ref.shape[1:]
    wide_ref[...] = jnp.zeros_like(wide_ref)
    wide_ref[0, :occupied, :] = green_ref[0, :, :LANES].astype(F32)
    wide_ref[1, :occupied, : orbitals - LANES] = green_ref[0, :, LANES:].astype(F32)
    rest = [wide_ref[1, t * TILE : (t + 1) * TILE, :] for t in range(STRIDE // TILE)]
    row, lane = tile_iotas()
    folded = [jnp.where(lane < HALF, rest[t], turned(rest[t + 3], HALF)) for t in range(3)]
    last, after = wide_ref[0, SIDE:STRIDE, :], rest[6]
    side = turned(last, SIDE)
    side = jnp.where((row == 2) | (row == 3), jnp.where(lane < 96, turned(last, -32, 2), turned(after, 56, 2)), side)
    side = jnp.where(row == 4, jnp.where(lane < 88, turned(after, SIDE, 4), turned(after, 88, 3)), side)
    for t in range(6):
        side = jnp.where((lane >= t * TILE) & (lane < (t + 1) * TILE), turned(rest[t], t * TILE - HALF), side)
    whole = wide_ref[0, :SIDE, :]
    noise = noise_ref[...]
    for slot, block in enumerate(order):
        piece = noise[:, block * slab : (block + 1) * slab]
        piece = jnp.concatenate([jnp.zeros((1, SIDE), F32), piece, jnp.zeros((1, LANES - SIDE - slab), F32)], axis=1)
        final = side
        for k, part in enumerate(split_three(piece)):
            final = jnp.where((row == 5 + k) & (lane >= SIDE), part.astype(F32), final)
        packed_ref[slot] = jnp.concatenate([whole, *folded, final], axis=0).astype(BF16)


def unpack(packed, rows_ref, at):
    row, lane = tile_iotas()
    side = packed[MESSAGE - TILE :]
    rows_ref[0, at : at + SIDE, :] = packed[:SIDE]
    for t in range(6):
        place = SIDE + (t % 3) * TILE
        tile = turned(packed[place : place + TILE], HALF if t >= 3 else 0)
        rows_ref[1, at + t * TILE : at + (t + 1) * TILE, :] = jnp.where(lane < HALF, tile, turned(side, HALF - t * TILE))
    first = turned(side, -SIDE)
    rows_ref[0, at + SIDE : at + STRIDE, :] = jnp.where((row >= 5) | (lane < 80), first, turned(side, 32, -2))
    tail = jnp.where(row == 0, turned(first, 0, -4), turned(side, -88, -3))
    rows_ref[1, at + SIDE : at + STRIDE, :] = jnp.where(lane < 40, tail, turned(side, -56, -2))


def plan_of(occupied):
    tiles = [("pair", p) for p in range(-(-occupied // 2))]
    tiles += [("eight", e) for e in range(-(-occupied // TILE))]
    tiles = tiles[::-1]
    place = {tile: divmod(k, 2) for k, tile in enumerate(tiles)}
    pairs = [place["pair", p] for p in range(-(-occupied // 2))]
    eights = [place["eight", e] for e in range(-(-occupied // TILE))]
    return pairs, eights, -(-len(tiles) // 2)


def prepare_kernel(slab, chol_ref, rhs_ref):
    occupied = chol_ref.shape[0]
    pairs, eights, products = plan_of(occupied)
    for p, t in eights + [(products - 1, 1)]:
        rhs_ref[p, t * LANES : (t + 1) * LANES, :] = jnp.zeros((LANES, rhs_ref.shape[2]), BF16)
    for i in range(occupied):
        p, t = pairs[i // 2]
        start = t * LANES + i % 2 * HALF
        rhs_ref[p, start : start + HALF, :] = chol_ref[i, :HALF, :]
        p, t = eights[i // TILE]
        start = t * LANES + i % TILE * SLOT
        rhs_ref[p, start : start + slab - HALF, :] = chol_ref[i, HALF:, :]


def tables_of(lhs, rhs_ref, table_ref):
    occupied = lhs.shape[0] // GROUP
    pairs, eights, products = plan_of(occupied)
    _, lane = tile_iotas()
    low = lane < HALF
    zero = jnp.zeros((GROUP, LANES), F32)
    at = {place: ("pair", k) for k, place in enumerate(pairs)} | {place: ("eight", k) for k, place in enumerate(eights)}

    def tile(place, j):
        if j >= occupied:
            return zero
        p, t = place
        return table_ref[p, j * GROUP : (j + 1) * GROUP, t * LANES : (t + 1) * LANES]

    def diagonals(tiles):
        for d in (1, 2, 4):
            keep = (lane // SLOT) & d == 0
            tiles = [jnp.where(keep, tiles[r], tiles[(r + d) % TILE]) for r in range(TILE)]
        return tiles

    def products_of(mine, other):
        return [mine[r] * turned(other[-r % TILE], -r * SLOT) for r in range(TILE)]

    once, twice = [zero] * 2, [zero] * 4
    trace, ends = [zero] * 2, zero
    done = {"pair": [], "eight": []}
    for p in range(products):
        table_ref[p] = lax.dot_general(lhs, rhs_ref[p], (((1,), (1,)), ((), ())), preferred_element_type=F32)
        for t in range(2):
            kind, k = at.get((p, t), (None, 0))
            if kind == "pair":
                for q in done[kind]:
                    mine = [tile(pairs[k], 2 * q), tile(pairs[k], 2 * q + 1)]
                    other = [tile(pairs[q], 2 * k), tile(pairs[q], 2 * k + 1)]
                    twice[0] += jnp.where(low, mine[0], mine[1]) * jnp.where(low, other[0], other[1])
                    twice[1] += jnp.where(low, mine[1], mine[0]) * turned(jnp.where(low, other[1], other[0]), HALF)
                mine = [tile(pairs[k], 2 * k), tile(pairs[k], 2 * k + 1)]
                both = jnp.where(low, mine[0], mine[1])
                trace[k % 2] += both
                once[0] += both * both
                twice[2] += jnp.where(low, turned(mine[0], HALF) * mine[1], 0.0)
                done[kind].append(k)
            elif kind == "eight":
                mine = diagonals([tile(eights[k], TILE * k + j) for j in range(TILE)])
                ends += mine[0]
                for product in products_of(mine, mine):
                    once[1] += product
                for q in done[kind]:
                    mine = diagonals([tile(eights[k], TILE * q + j) for j in range(TILE)])
                    other = diagonals([tile(eights[q], TILE * k + j) for j in range(TILE)])
                    for product in products_of(mine, other):
                        twice[3] += product
                done[kind].append(k)
    trace = trace[0] + trace[1]
    trace = trace + turned(trace, HALF)
    for lanes in (HALF, HALF // 2, HALF // 4):
        ends = ends + turned(ends, lanes)
    total = once[0] + once[1] + 2.0 * ((twice[0] + twice[1]) + (twice[2] + twice[3]))
    return jnp.where(low, trace, ends), total


def work_kernel(slab, order, offsets, walk, arrived_ref, rhs_ref, body_ref, old_ref, send_ref, rows_ref, lhs_ref, table_ref):
    blocks = arrived_ref.shape[0]
    occupied, orbitals = body_ref.shape
    rows = STRIDE
    folds = send_ref.shape[0] // (blocks * walk)
    wide = folds * LANES
    at_energy, at_exponent, at_old, at_kinetic = offsets
    chunks = [(low, min(low + LANES, orbitals)) for low in range(0, orbitals, LANES)]
    own = lax.axis_index("blk")
    kinetic = jnp.zeros((1, 1), F32)
    force, cross, noise = [], [], []
    lane = lax.broadcasted_iota(jnp.int32, (GROUP, LANES), 1)
    for first in range(0, blocks, GROUP):
        for w in range(GROUP):
            unpack(arrived_ref[order.index(first + w)].astype(F32), rows_ref, w * rows)
        for j in range(0, occupied, 2):
            for c, (low, high) in enumerate(chunks):
                pair = [rows_ref[c, pl.ds(j + k, GROUP, stride=rows), :] for k in range(2)]
                pair = jnp.concatenate(pair, axis=0).astype(BF16)
                lhs_ref[j * GROUP : (j + 2) * GROUP, low:high] = pair[:, : high - low]
        place = pl.multiple_of(lax.rem(own, GROUP) * rows, TILE)
        here = jnp.zeros((1, 1), F32)
        for c, (low, high) in enumerate(chunks):
            mine = rows_ref[c, pl.ds(place, occupied), :][:, : high - low]
            here += jnp.sum(mine * body_ref[:, low:high], axis=(0, 1), keepdims=True)
        kinetic = jnp.where(own // GROUP == first // GROUP, here, kinetic)
        parts = [rows_ref[0, pl.ds(rows - 3 + k, GROUP, stride=rows), :] for k in range(3)]
        noise.append((parts[0] + parts[1]) + parts[2])
        trace, total = tables_of(lhs_ref[...], rhs_ref, table_ref)
        force.append(jnp.where(lane < slab, trace, 0.0))
        cross.append(total)
    force = jnp.concatenate(force, axis=0)
    cross = jnp.concatenate(cross, axis=0)
    noise = jnp.concatenate(noise, axis=0)
    in_slab = lax.broadcasted_iota(jnp.int32, (blocks, LANES), 1) < slab
    shifted = F32(-0.1) * force
    gain = jnp.where(in_slab, noise * shifted + 0.5 * shifted * shifted, 0.0)
    energy = jnp.sum(0.5 * force * force - 0.5 * cross, axis=1, keepdims=True)
    exponent = jnp.sum(gain, axis=1, keepdims=True) - 0.01 * energy
    if wide > LANES:
        force = jnp.concatenate([force, jnp.zeros((blocks, wide - LANES), F32)], axis=1)
    lane = lax.broadcasted_iota(jnp.int32, (blocks, wide), 1)
    row = lax.broadcasted_iota(jnp.int32, (blocks, wide), 0)
    across = jnp.sum(jnp.where(lane - at_exponent == row, exponent, 0.0), axis=0, keepdims=True)
    message = jnp.where(lane < at_energy, force, energy)
    message = jnp.where(lane >= at_exponent, across, message)
    message = jnp.where(lane >= at_old, old_ref[...], message)
    message = jnp.where(lane >= at_kinetic, kinetic, message)
    for k in range(walk * folds):
        c = k % folds
        send_ref[pl.ds(k, blocks, stride=walk * folds), :] = message[:, c * LANES : (c + 1) * LANES]


def finish_kernel(slab, offsets, blocks, walk, got_ref, force_ref, energy_ref, weight_ref, comb_ref):
    folds = got_ref.shape[0] // (blocks * walk)
    wide = folds * LANES
    at_energy, at_exponent, at_old, at_kinetic = offsets
    own_block = lax.axis_index("blk")
    own_walk = lax.axis_index("walk")
    lane = lax.broadcasted_iota(jnp.int32, (blocks, wide), 1)
    row = lax.broadcasted_iota(jnp.int32, (blocks, wide), 0)
    keep = (lane < at_old) | (lane - at_old == row) | (lane - at_kinetic == row)
    own = jnp.zeros((blocks, wide), F32)
    sums = []
    for w in range(walk):
        from_w = [got_ref[pl.ds(w * folds + c, blocks, stride=walk * folds), :] for c in range(folds)]
        from_w = jnp.concatenate(from_w, axis=1)
        own = jnp.where(own_walk == w, from_w, own)
        sums.append(jnp.sum(jnp.where(keep, from_w, 0.0), axis=0, keepdims=True))
    for b in range(blocks):
        force_ref[:, b * slab : (b + 1) * slab] = own[b : b + 1, :slab]
    sums = jnp.concatenate(sums, axis=0)
    exponent = sums[:, at_exponent : at_exponent + blocks]
    old = sums[:, at_old : at_old + blocks]
    kinetic = sums[:, at_kinetic : at_kinetic + blocks]
    weight = old * jnp.exp(exponent - 0.01 * kinetic)
    index = lax.broadcasted_iota(jnp.int32, (walk, blocks), 1) * walk + lax.broadcasted_iota(jnp.int32, (walk, blocks), 0)
    rank = own_block * walk + own_walk

    def total(values):
        return jnp.sum(values, axis=(0, 1), keepdims=True)

    before = total(jnp.where(index < rank, weight, 0.0))
    weight_ref[...] = total(jnp.where(index == rank, weight, 0.0))
    energy_ref[...] = total(jnp.where(lane == at_energy, own, 0.0)) + total(jnp.where(index == rank, kinetic, 0.0))
    comb_ref[...] = before * (blocks * walk) / total(weight) - rank.astype(F32)


def on_device(green_half, chol_half, one_body, field_noise, old_weight):
    slab, occupied, orbitals = chol_half.shape
    blocks = lax.axis_size("blk")
    walk = lax.axis_size("walk")
    order = exchange_order(blocks)
    vmem = pl.BlockSpec(memory_space=pltpu.VMEM)
    products = plan_of(occupied)[2]
    small = pltpu.CompilerParams(vmem_limit_bytes=4 * 2**20)
    message = (blocks, MESSAGE, LANES)
    packed = pl.pallas_call(
        functools.partial(pack_kernel, slab, order),
        out_shape=jax.ShapeDtypeStruct(message, BF16),
        in_specs=[vmem, vmem],
        out_specs=vmem,
        scratch_shapes=[pltpu.VMEM((2, STRIDE, LANES), F32)],
        compiler_params=pltpu.CompilerParams(vmem_limit_bytes=60 * 2**20),
        name="pack",
    )(green_half, field_noise)
    arrived = lax.all_to_all(packed, "blk", split_axis=0, concat_axis=0, axis_index_groups=[order], tiled=True)
    rhs = pl.pallas_call(
        functools.partial(prepare_kernel, slab),
        out_shape=jax.ShapeDtypeStruct((products, 2 * LANES, orbitals), BF16),
        in_specs=[vmem],
        out_specs=vmem,
        compiler_params=pltpu.CompilerParams(vmem_limit_bytes=12 * 2**20),
        name="prepare",
    )(jnp.swapaxes(chol_half, 0, 1))
    offsets = (slab, slab + 1, slab + 1 + blocks, slab + 1 + 2 * blocks)
    folds = round_up(slab + 1 + 3 * blocks, LANES) // LANES
    send = pl.pallas_call(
        functools.partial(work_kernel, slab, order, offsets, walk),
        out_shape=jax.ShapeDtypeStruct((blocks * walk * folds, LANES), F32),
        in_specs=[vmem] * 4,
        out_specs=vmem,
        scratch_shapes=[
            pltpu.VMEM((round_up(orbitals, LANES) // LANES, GROUP * STRIDE, LANES), F32),
            pltpu.VMEM((GROUP * occupied, orbitals), BF16),
            pltpu.VMEM((products, GROUP * occupied, 2 * LANES), F32),
        ],
        compiler_params=pltpu.CompilerParams(vmem_limit_bytes=32 * 2**20),
        name="work",
    )(arrived, rhs, one_body, old_weight.reshape(1, 1))
    got = lax.all_to_all(send, ("blk", "walk"), split_axis=0, concat_axis=0, tiled=True)
    one = jax.ShapeDtypeStruct((1, 1), F32)
    force, energy, weight, comb = pl.pallas_call(
        functools.partial(finish_kernel, slab, offsets, blocks, walk),
        out_shape=(jax.ShapeDtypeStruct((1, slab * blocks), F32), one, one, one),
        in_specs=[vmem],
        out_specs=(vmem,) * 4,
        compiler_params=small,
        name="finish",
    )(got)
    return force, energy.reshape(1), weight.reshape(1), comb.reshape(1)


def solution(mesh):
    placed = (
        P(("blk", "walk"), None, None),
        P("blk", None, None),
        P(),
        P(("blk", "walk"), None),
        P(("blk", "walk")),
    )
    return jax.shard_map(
        on_device,
        mesh=mesh,
        in_specs=placed,
        out_specs=(
            P(("blk", "walk"), None),
            P(("blk", "walk")),
            P(("blk", "walk")),
            P(("blk", "walk")),
        ),
        check_vma=False,
    )
```

```python
import functools

import jax
import jax.numpy as jnp
from jax import lax
from jax.experimental import pallas as pl
from jax.experimental.pallas import tpu as pltpu
from jax.sharding import PartitionSpec as P

F32 = jnp.float32
BF16 = jnp.bfloat16
LANES = 128
TILE = 8
HALF = LANES // 2
SLOT = LANES // TILE
GROUP = 8


def round_up(value, unit):
    return -(-value // unit) * unit


def split_three(values):
    high = values.astype(BF16)
    rest = values - high.astype(F32)
    middle = rest.astype(BF16)
    low = (rest - middle.astype(F32)).astype(BF16)
    return high, middle, low


def exchange_order(blocks):
    if blocks % 2:
        return list(range(blocks))
    half = blocks // 2
    return [block for low in [half - 1, *range(half - 1)] for block in (low, low + half)]


MESSAGE = 80
STRIDE = 56
SIDE = 48


def tile_iotas():
    shape = (TILE, LANES)
    return lax.broadcasted_iota(jnp.int32, shape, 0), lax.broadcasted_iota(jnp.int32, shape, 1)


def turned(tile, lanes=0, rows=0):
    tile = pltpu.roll(tile, lanes % LANES, 1) if lanes % LANES else tile
    return pltpu.roll(tile, rows % TILE, 0) if rows % TILE else tile


def pack_kernel(slab, order, green_ref, noise_ref, packed_ref, wide_ref):
    occupied, orbitals = green_ref.shape[1:]
    wide_ref[...] = jnp.zeros_like(wide_ref)
    wide_ref[0, :occupied, :] = green_ref[0, :, :LANES].astype(F32)
    wide_ref[1, :occupied, : orbitals - LANES] = green_ref[0, :, LANES:].astype(F32)
    rest = [wide_ref[1, t * TILE : (t + 1) * TILE, :] for t in range(STRIDE // TILE)]
    row, lane = tile_iotas()
    folded = [jnp.where(lane < HALF, rest[t], turned(rest[t + 3], HALF)) for t in range(3)]
    last, after = wide_ref[0, SIDE:STRIDE, :], rest[6]
    side = turned(last, SIDE)
    side = jnp.where((row == 2) | (row == 3), jnp.where(lane < 96, turned(last, -32, 2), turned(after, 56, 2)), side)
    side = jnp.where(row == 4, jnp.where(lane < 88, turned(after, SIDE, 4), turned(after, 88, 3)), side)
    for t in range(6):
        side = jnp.where((lane >= t * TILE) & (lane < (t + 1) * TILE), turned(rest[t], t * TILE - HALF), side)
    whole = green_ref[0, :SIDE, :LANES].astype(F32)
    noise = noise_ref[...]
    for slot, block in enumerate(order):
        piece = noise[:, block * slab : (block + 1) * slab]
        piece = jnp.concatenate([jnp.zeros((1, SIDE), F32), piece, jnp.zeros((1, LANES - SIDE - slab), F32)], axis=1)
        final = side
        for k, part in enumerate(split_three(piece)):
            final = jnp.where((row == 5 + k) & (lane >= SIDE), part.astype(F32), final)
        packed_ref[slot] = jnp.concatenate([whole, *folded, final], axis=0).astype(BF16)


def unpack(packed, rows_ref, at):
    row, lane = tile_iotas()
    side = packed[MESSAGE - TILE :]
    rows_ref[0, at : at + SIDE, :] = packed[:SIDE]
    for t in range(6):
        place = SIDE + (t % 3) * TILE
        tile = turned(packed[place : place + TILE], HALF if t >= 3 else 0)
        rows_ref[1, at + t * TILE : at + (t + 1) * TILE, :] = jnp.where(lane < HALF, tile, turned(side, HALF - t * TILE))
    first = turned(side, -SIDE)
    rows_ref[0, at + SIDE : at + STRIDE, :] = jnp.where((row >= 5) | (lane < 80), first, turned(side, 32, -2))
    tail = jnp.where(row == 0, turned(first, 0, -4), turned(side, -88, -3))
    rows_ref[1, at + SIDE : at + STRIDE, :] = jnp.where(lane < 40, tail, turned(side, -56, -2))


def plan_of(occupied):
    tiles = [("pair", p) for p in range(-(-occupied // 2))]
    tiles += [("eight", e) for e in range(-(-occupied // TILE))]
    tiles = tiles[::-1]
    place = {tile: divmod(k, 2) for k, tile in enumerate(tiles)}
    pairs = [place["pair", p] for p in range(-(-occupied // 2))]
    eights = [place["eight", e] for e in range(-(-occupied // TILE))]
    return pairs, eights, -(-len(tiles) // 2)


def prepare_kernel(slab, chol_ref, rhs_ref):
    occupied = chol_ref.shape[0]
    pairs, eights, products = plan_of(occupied)
    for p, t in eights + [(products - 1, 1)]:
        rhs_ref[p, t * LANES : (t + 1) * LANES, :] = jnp.zeros((LANES, rhs_ref.shape[2]), BF16)
    for i in range(occupied):
        p, t = pairs[i // 2]
        start = t * LANES + i % 2 * HALF
        rhs_ref[p, start : start + HALF, :] = chol_ref[i, :HALF, :]
        p, t = eights[i // TILE]
        start = t * LANES + i % TILE * SLOT
        rhs_ref[p, start : start + slab - HALF, :] = chol_ref[i, HALF:, :]


def tables_of(lhs, rhs_ref, table_ref):
    occupied = lhs.shape[0] // GROUP
    pairs, eights, products = plan_of(occupied)
    _, lane = tile_iotas()
    low = lane < HALF
    zero = jnp.zeros((GROUP, LANES), F32)
    at = {place: ("pair", k) for k, place in enumerate(pairs)} | {place: ("eight", k) for k, place in enumerate(eights)}

    def tile(place, j):
        if j >= occupied:
            return zero
        p, t = place
        return table_ref[p, j * GROUP : (j + 1) * GROUP, t * LANES : (t + 1) * LANES]

    def diagonals(tiles):
        for d in (1, 2, 4):
            keep = (lane // SLOT) & d == 0
            tiles = [jnp.where(keep, tiles[r], tiles[(r + d) % TILE]) for r in range(TILE)]
        return tiles

    def products_of(mine, other):
        return [mine[r] * turned(other[-r % TILE], -r * SLOT) for r in range(TILE)]

    once, twice = [zero] * 2, [zero] * 4
    trace, ends = [zero] * 2, zero
    done = {"pair": [], "eight": []}
    for p in range(products):
        table_ref[p] = lax.dot_general(lhs, rhs_ref[p], (((1,), (1,)), ((), ())), preferred_element_type=F32)
        for t in range(2):
            kind, k = at.get((p, t), (None, 0))
            if kind == "pair":
                for q in done[kind]:
                    mine = [tile(pairs[k], 2 * q), tile(pairs[k], 2 * q + 1)]
                    other = [tile(pairs[q], 2 * k), tile(pairs[q], 2 * k + 1)]
                    twice[0] += jnp.where(low, mine[0], mine[1]) * jnp.where(low, other[0], other[1])
                    twice[1] += jnp.where(low, mine[1], mine[0]) * turned(jnp.where(low, other[1], other[0]), HALF)
                mine = [tile(pairs[k], 2 * k), tile(pairs[k], 2 * k + 1)]
                both = jnp.where(low, mine[0], mine[1])
                trace[k % 2] += both
                once[0] += both * both
                twice[2] += jnp.where(low, turned(mine[0], HALF) * mine[1], 0.0)
                done[kind].append(k)
            elif kind == "eight":
                mine = diagonals([tile(eights[k], TILE * k + j) for j in range(TILE)])
                ends += mine[0]
                for product in products_of(mine, mine):
                    once[1] += product
                for q in done[kind]:
                    mine = diagonals([tile(eights[k], TILE * q + j) for j in range(TILE)])
                    other = diagonals([tile(eights[q], TILE * k + j) for j in range(TILE)])
                    for product in products_of(mine, other):
                        twice[3] += product
                done[kind].append(k)
    trace = trace[0] + trace[1]
    trace = trace + turned(trace, HALF)
    for lanes in (HALF, HALF // 2, HALF // 4):
        ends = ends + turned(ends, lanes)
    total = once[0] + once[1] + 2.0 * ((twice[0] + twice[1]) + (twice[2] + twice[3]))
    return jnp.where(low, trace, ends), total


def work_kernel(slab, order, offsets, walk, arrived_ref, rhs_ref, body_ref, old_ref, send_ref, rows_ref, lhs_ref, table_ref):
    blocks = arrived_ref.shape[0]
    occupied, orbitals = body_ref.shape
    rows = STRIDE
    folds = send_ref.shape[0] // (blocks * walk)
    wide = folds * LANES
    at_energy, at_exponent, at_old, at_kinetic = offsets
    chunks = [(low, min(low + LANES, orbitals)) for low in range(0, orbitals, LANES)]
    own = lax.axis_index("blk")
    kinetic = jnp.zeros((1, 1), F32)
    force, cross, noise = [], [], []
    lane = lax.broadcasted_iota(jnp.int32, (GROUP, LANES), 1)
    for first in range(0, blocks, GROUP):
        for w in range(GROUP):
            unpack(arrived_ref[order.index(first + w)].astype(F32), rows_ref, w * rows)
        for j in range(0, occupied, 2):
            for c, (low, high) in enumerate(chunks):
                pair = [rows_ref[c, pl.ds(j + k, GROUP, stride=rows), :] for k in range(2)]
                pair = jnp.concatenate(pair, axis=0).astype(BF16)
                lhs_ref[j * GROUP : (j + 2) * GROUP, low:high] = pair[:, : high - low]
        place = pl.multiple_of(lax.rem(own, GROUP) * rows, TILE)
        here = jnp.zeros((1, 1), F32)
        for c, (low, high) in enumerate(chunks):
            mine = rows_ref[c, pl.ds(place, occupied), :][:, : high - low]
            here += jnp.sum(mine * body_ref[:, low:high], axis=(0, 1), keepdims=True)
        kinetic = jnp.where(own // GROUP == first // GROUP, here, kinetic)
        parts = [rows_ref[0, pl.ds(rows - 3 + k, GROUP, stride=rows), :] for k in range(3)]
        noise.append((parts[0] + parts[1]) + parts[2])
        trace, total = tables_of(lhs_ref[...], rhs_ref, table_ref)
        force.append(jnp.where(lane < slab, trace, 0.0))
        cross.append(total)
    force = jnp.concatenate(force, axis=0)
    cross = jnp.concatenate(cross, axis=0)
    noise = jnp.concatenate(noise, axis=0)
    in_slab = lax.broadcasted_iota(jnp.int32, (blocks, LANES), 1) < slab
    shifted = F32(-0.1) * force
    gain = jnp.where(in_slab, noise * shifted + 0.5 * shifted * shifted, 0.0)
    energy = jnp.sum(0.5 * force * force - 0.5 * cross, axis=1, keepdims=True)
    exponent = jnp.sum(gain, axis=1, keepdims=True) - 0.01 * energy
    if wide > LANES:
        force = jnp.concatenate([force, jnp.zeros((blocks, wide - LANES), F32)], axis=1)
    lane = lax.broadcasted_iota(jnp.int32, (blocks, wide), 1)
    row = lax.broadcasted_iota(jnp.int32, (blocks, wide), 0)
    across = jnp.sum(jnp.where(lane - at_exponent == row, exponent, 0.0), axis=0, keepdims=True)
    message = jnp.where(lane < at_energy, force, energy)
    message = jnp.where(lane >= at_exponent, across, message)
    message = jnp.where(lane >= at_old, old_ref[...], message)
    message = jnp.where(lane >= at_kinetic, kinetic, message)
    for k in range(walk * folds):
        c = k % folds
        send_ref[pl.ds(k, blocks, stride=walk * folds), :] = message[:, c * LANES : (c + 1) * LANES]


def finish_kernel(slab, offsets, blocks, walk, got_ref, force_ref, energy_ref, weight_ref, comb_ref):
    folds = got_ref.shape[0] // (blocks * walk)
    wide = folds * LANES
    at_energy, at_exponent, at_old, at_kinetic = offsets
    own_block = lax.axis_index("blk")
    own_walk = lax.axis_index("walk")
    lane = lax.broadcasted_iota(jnp.int32, (blocks, wide), 1)
    row = lax.broadcasted_iota(jnp.int32, (blocks, wide), 0)
    keep = (lane < at_old) | (lane - at_old == row) | (lane - at_kinetic == row)
    own = jnp.zeros((blocks, wide), F32)
    sums = []
    for w in range(walk):
        from_w = [got_ref[pl.ds(w * folds + c, blocks, stride=walk * folds), :] for c in range(folds)]
        from_w = jnp.concatenate(from_w, axis=1)
        own = jnp.where(own_walk == w, from_w, own)
        sums.append(jnp.sum(jnp.where(keep, from_w, 0.0), axis=0, keepdims=True))
    for b in range(blocks):
        force_ref[:, b * slab : (b + 1) * slab] = own[b : b + 1, :slab]
    sums = jnp.concatenate(sums, axis=0)
    place = lax.broadcasted_iota(jnp.int32, (walk, wide), 1) - at_exponent
    inside = (place >= 0) & (place < blocks)
    old = pltpu.roll(sums, wide - (at_old - at_exponent), 1)
    kinetic = pltpu.roll(sums, wide - (at_kinetic - at_exponent), 1)
    change = jnp.where(inside, sums - 0.01 * kinetic, 0.0)
    weight = jnp.where(inside, old * jnp.exp(change), 0.0)
    index = place * walk + lax.broadcasted_iota(jnp.int32, (walk, wide), 0)
    rank = own_block * walk + own_walk

    def total(values):
        return jnp.sum(values, axis=(0, 1), keepdims=True)

    before = total(jnp.where(index < rank, weight, 0.0))
    weight_ref[...] = total(jnp.where(index == rank, weight, 0.0))
    energy_ref[...] = total(jnp.where(lane == at_energy, own, 0.0)) + total(jnp.where(inside & (index == rank), kinetic, 0.0))
    comb_ref[...] = before * (blocks * walk) / total(weight) - rank.astype(F32)


def on_device(green_half, chol_half, one_body, field_noise, old_weight):
    slab, occupied, orbitals = chol_half.shape
    blocks = lax.axis_size("blk")
    walk = lax.axis_size("walk")
    order = exchange_order(blocks)
    vmem = pl.BlockSpec(memory_space=pltpu.VMEM)
    products = plan_of(occupied)[2]
    small = pltpu.CompilerParams(vmem_limit_bytes=4 * 2**20)
    message = (blocks, MESSAGE, LANES)
    packed = pl.pallas_call(
        functools.partial(pack_kernel, slab, order),
        out_shape=jax.ShapeDtypeStruct(message, BF16),
        in_specs=[vmem, vmem],
        out_specs=vmem,
        scratch_shapes=[pltpu.VMEM((2, STRIDE, LANES), F32)],
        compiler_params=pltpu.CompilerParams(vmem_limit_bytes=60 * 2**20),
        name="pack",
    )(green_half, field_noise)
    arrived = lax.all_to_all(packed, "blk", split_axis=0, concat_axis=0, axis_index_groups=[order], tiled=True)
    rhs = pl.pallas_call(
        functools.partial(prepare_kernel, slab),
        out_shape=jax.ShapeDtypeStruct((products, 2 * LANES, orbitals), BF16),
        in_specs=[vmem],
        out_specs=vmem,
        compiler_params=pltpu.CompilerParams(vmem_limit_bytes=12 * 2**20),
        name="prepare",
    )(jnp.swapaxes(chol_half, 0, 1))
    offsets = (slab, slab + 1, slab + 1 + blocks, slab + 1 + 2 * blocks)
    folds = round_up(slab + 1 + 3 * blocks, LANES) // LANES
    send = pl.pallas_call(
        functools.partial(work_kernel, slab, order, offsets, walk),
        out_shape=jax.ShapeDtypeStruct((blocks * walk * folds, LANES), F32),
        in_specs=[vmem] * 4,
        out_specs=vmem,
        scratch_shapes=[
            pltpu.VMEM((round_up(orbitals, LANES) // LANES, GROUP * STRIDE, LANES), F32),
            pltpu.VMEM((GROUP * occupied, orbitals), BF16),
            pltpu.VMEM((products, GROUP * occupied, 2 * LANES), F32),
        ],
        compiler_params=pltpu.CompilerParams(vmem_limit_bytes=32 * 2**20),
        name="work",
    )(arrived, rhs, one_body, old_weight.reshape(1, 1))
    got = lax.all_to_all(send, ("blk", "walk"), split_axis=0, concat_axis=0, tiled=True)
    one = jax.ShapeDtypeStruct((1, 1), F32)
    force, energy, weight, comb = pl.pallas_call(
        functools.partial(finish_kernel, slab, offsets, blocks, walk),
        out_shape=(jax.ShapeDtypeStruct((1, slab * blocks), F32), one, one, one),
        in_specs=[vmem],
        out_specs=(vmem,) * 4,
        compiler_params=small,
        name="finish",
    )(got)
    return force, energy.reshape(1), weight.reshape(1), comb.reshape(1)


def solution(mesh):
    placed = (
        P(("blk", "walk"), None, None),
        P("blk", None, None),
        P(),
        P(("blk", "walk"), None),
        P(("blk", "walk")),
    )
    return jax.shard_map(
        on_device,
        mesh=mesh,
        in_specs=placed,
        out_specs=(
            P(("blk", "walk"), None),
            P(("blk", "walk")),
            P(("blk", "walk")),
            P(("blk", "walk")),
        ),
        check_vma=False,
    )
```

```python
import functools

import jax
import jax.numpy as jnp
from jax import lax
from jax.experimental import pallas as pl
from jax.experimental.pallas import tpu as pltpu
from jax.sharding import PartitionSpec as P

F32 = jnp.float32
BF16 = jnp.bfloat16
LANES = 128
TILE = 8
HALF = LANES // 2
SLOT = LANES // TILE
GROUP = 8


def round_up(value, unit):
    return -(-value // unit) * unit


def split_three(values):
    high = values.astype(BF16)
    rest = values - high.astype(F32)
    middle = rest.astype(BF16)
    low = (rest - middle.astype(F32)).astype(BF16)
    return high, middle, low


def exchange_order(blocks):
    if blocks % 2:
        return list(range(blocks))
    half = blocks // 2
    return [block for low in [half - 1, *range(half - 1)] for block in (low, low + half)]


MESSAGE = 80
STRIDE = 56
SIDE = 48


def tile_iotas():
    shape = (TILE, LANES)
    return lax.broadcasted_iota(jnp.int32, shape, 0), lax.broadcasted_iota(jnp.int32, shape, 1)


def turned(tile, lanes=0, rows=0):
    tile = pltpu.roll(tile, lanes % LANES, 1) if lanes % LANES else tile
    return pltpu.roll(tile, rows % TILE, 0) if rows % TILE else tile


def pack_kernel(slab, order, green_ref, noise_ref, packed_ref, wide_ref):
    occupied, orbitals = green_ref.shape[1:]
    wide_ref[...] = jnp.zeros_like(wide_ref)
    wide_ref[0, :occupied, :] = green_ref[0, :, :LANES].astype(F32)
    wide_ref[1, :occupied, : orbitals - LANES] = green_ref[0, :, LANES:].astype(F32)
    rest = [wide_ref[1, t * TILE : (t + 1) * TILE, :] for t in range(STRIDE // TILE)]
    row, lane = tile_iotas()
    folded = [jnp.where(lane < HALF, rest[t], turned(rest[t + 3], HALF)) for t in range(3)]
    last, after = wide_ref[0, SIDE:STRIDE, :], rest[6]
    side = turned(last, SIDE)
    side = jnp.where((row == 2) | (row == 3), jnp.where(lane < 96, turned(last, -32, 2), turned(after, 56, 2)), side)
    side = jnp.where(row == 4, jnp.where(lane < 88, turned(after, SIDE, 4), turned(after, 88, 3)), side)
    for t in range(6):
        side = jnp.where((lane >= t * TILE) & (lane < (t + 1) * TILE), turned(rest[t], t * TILE - HALF), side)
    whole = green_ref[0, :SIDE, :LANES].astype(F32)
    noise = noise_ref[...]
    for slot, block in enumerate(order):
        piece = noise[:, block * slab : (block + 1) * slab]
        piece = jnp.concatenate([jnp.zeros((1, SIDE), F32), piece, jnp.zeros((1, LANES - SIDE - slab), F32)], axis=1)
        final = side
        for k, part in enumerate(split_three(piece)):
            final = jnp.where((row == 5 + k) & (lane >= SIDE), part.astype(F32), final)
        packed_ref[slot] = jnp.concatenate([whole, *folded, final], axis=0).astype(BF16)


def unpack(packed, rows_ref, at):
    row, lane = tile_iotas()
    side = packed[MESSAGE - TILE :]
    rows_ref[0, at : at + SIDE, :] = packed[:SIDE]
    for t in range(6):
        place = SIDE + (t % 3) * TILE
        tile = turned(packed[place : place + TILE], HALF if t >= 3 else 0)
        rows_ref[1, at + t * TILE : at + (t + 1) * TILE, :] = jnp.where(lane < HALF, tile, turned(side, HALF - t * TILE))
    first = turned(side, -SIDE)
    rows_ref[0, at + SIDE : at + STRIDE, :] = jnp.where((row >= 5) | (lane < 80), first, turned(side, 32, -2))
    tail = jnp.where(row == 0, turned(first, 0, -4), turned(side, -88, -3))
    rows_ref[1, at + SIDE : at + STRIDE, :] = jnp.where(lane < 40, tail, turned(side, -56, -2))


def plan_of(occupied):
    tiles = [("pair", p) for p in range(-(-occupied // 2))]
    middle = TILE + 1
    tiles[middle:middle] = [("eight", e) for e in range(-(-occupied // TILE))]
    place = {tile: divmod(k, 2) for k, tile in enumerate(tiles)}
    pairs = [place["pair", p] for p in range(-(-occupied // 2))]
    eights = [place["eight", e] for e in range(-(-occupied // TILE))]
    return pairs, eights, -(-len(tiles) // 2)


def prepare_kernel(slab, chol_ref, rhs_ref):
    occupied = chol_ref.shape[0]
    pairs, eights, products = plan_of(occupied)
    for p, t in eights + [(products - 1, 1)]:
        rhs_ref[p, t * LANES : (t + 1) * LANES, :] = jnp.zeros((LANES, rhs_ref.shape[2]), BF16)
    for i in range(occupied):
        p, t = pairs[i // 2]
        start = t * LANES + i % 2 * HALF
        rhs_ref[p, start : start + HALF, :] = chol_ref[i, :HALF, :]
        p, t = eights[i // TILE]
        start = t * LANES + i % TILE * SLOT
        rhs_ref[p, start : start + slab - HALF, :] = chol_ref[i, HALF:, :]


def tables_of(lhs, rhs_ref, table_ref):
    occupied = lhs.shape[0] // GROUP
    pairs, eights, products = plan_of(occupied)
    _, lane = tile_iotas()
    low = lane < HALF
    zero = jnp.zeros((GROUP, LANES), F32)
    at = {place: ("pair", k) for k, place in enumerate(pairs)} | {place: ("eight", k) for k, place in enumerate(eights)}

    def tile(place, j):
        if j >= occupied:
            return zero
        p, t = place
        return table_ref[p, j * GROUP : (j + 1) * GROUP, t * LANES : (t + 1) * LANES]

    def diagonals(tiles):
        for d in (1, 2, 4):
            keep = (lane // SLOT) & d == 0
            tiles = [jnp.where(keep, tiles[r], tiles[(r + d) % TILE]) for r in range(TILE)]
        return tiles

    def products_of(mine, other):
        return [mine[r] * turned(other[-r % TILE], -r * SLOT) for r in range(TILE)]

    once, twice = [zero] * 2, [zero] * 4
    trace, ends = [zero] * 2, zero
    done = {"pair": [], "eight": []}
    for p in range(products):
        table_ref[p] = lax.dot_general(lhs, rhs_ref[p], (((1,), (1,)), ((), ())), preferred_element_type=F32)
        for t in range(2):
            kind, k = at.get((p, t), (None, 0))
            if kind == "pair":
                for q in done[kind]:
                    mine = [tile(pairs[k], 2 * q), tile(pairs[k], 2 * q + 1)]
                    other = [tile(pairs[q], 2 * k), tile(pairs[q], 2 * k + 1)]
                    twice[0] += jnp.where(low, mine[0], mine[1]) * jnp.where(low, other[0], other[1])
                    twice[1] += jnp.where(low, mine[1], mine[0]) * turned(jnp.where(low, other[1], other[0]), HALF)
                mine = [tile(pairs[k], 2 * k), tile(pairs[k], 2 * k + 1)]
                both = jnp.where(low, mine[0], mine[1])
                trace[k % 2] += both
                once[0] += both * both
                twice[2] += jnp.where(low, turned(mine[0], HALF) * mine[1], 0.0)
                done[kind].append(k)
            elif kind == "eight":
                mine = diagonals([tile(eights[k], TILE * k + j) for j in range(TILE)])
                ends += mine[0]
                for product in products_of(mine, mine):
                    once[1] += product
                for q in done[kind]:
                    mine = diagonals([tile(eights[k], TILE * q + j) for j in range(TILE)])
                    other = diagonals([tile(eights[q], TILE * k + j) for j in range(TILE)])
                    for product in products_of(mine, other):
                        twice[3] += product
                done[kind].append(k)
    trace = trace[0] + trace[1]
    trace = trace + turned(trace, HALF)
    for lanes in (HALF, HALF // 2, HALF // 4):
        ends = ends + turned(ends, lanes)
    total = once[0] + once[1] + 2.0 * ((twice[0] + twice[1]) + (twice[2] + twice[3]))
    return jnp.where(low, trace, ends), total


def work_kernel(slab, order, offsets, walk, arrived_ref, rhs_ref, body_ref, old_ref, send_ref, rows_ref, lhs_ref, table_ref):
    blocks = arrived_ref.shape[0]
    occupied, orbitals = body_ref.shape
    rows = STRIDE
    folds = send_ref.shape[0] // (blocks * walk)
    wide = folds * LANES
    at_energy, at_exponent, at_old, at_kinetic = offsets
    chunks = [(low, min(low + LANES, orbitals)) for low in range(0, orbitals, LANES)]
    own = lax.axis_index("blk")
    kinetic = jnp.zeros((1, 1), F32)
    force, cross, noise = [], [], []
    lane = lax.broadcasted_iota(jnp.int32, (GROUP, LANES), 1)
    for first in range(0, blocks, GROUP):
        for w in range(GROUP):
            unpack(arrived_ref[order.index(first + w)].astype(F32), rows_ref, w * rows)
        for j in range(0, occupied, 2):
            for c, (low, high) in enumerate(chunks):
                pair = [rows_ref[c, pl.ds(j + k, GROUP, stride=rows), :] for k in range(2)]
                pair = jnp.concatenate(pair, axis=0).astype(BF16)
                lhs_ref[j * GROUP : (j + 2) * GROUP, low:high] = pair[:, : high - low]
        place = pl.multiple_of(lax.rem(own, GROUP) * rows, TILE)
        here = jnp.zeros((1, 1), F32)
        for c, (low, high) in enumerate(chunks):
            mine = rows_ref[c, pl.ds(place, occupied), :][:, : high - low]
            here += jnp.sum(mine * body_ref[:, low:high], axis=(0, 1), keepdims=True)
        kinetic = jnp.where(own // GROUP == first // GROUP, here, kinetic)
        parts = [rows_ref[0, pl.ds(rows - 3 + k, GROUP, stride=rows), :] for k in range(3)]
        noise.append((parts[0] + parts[1]) + parts[2])
        trace, total = tables_of(lhs_ref[...], rhs_ref, table_ref)
        force.append(jnp.where(lane < slab, trace, 0.0))
        cross.append(total)
    force = jnp.concatenate(force, axis=0)
    cross = jnp.concatenate(cross, axis=0)
    noise = jnp.concatenate(noise, axis=0)
    in_slab = lax.broadcasted_iota(jnp.int32, (blocks, LANES), 1) < slab
    shifted = F32(-0.1) * force
    gain = jnp.where(in_slab, noise * shifted + 0.5 * shifted * shifted, 0.0)
    energy = jnp.sum(0.5 * force * force - 0.5 * cross, axis=1, keepdims=True)
    exponent = jnp.sum(gain, axis=1, keepdims=True) - 0.01 * energy
    if wide > LANES:
        force = jnp.concatenate([force, jnp.zeros((blocks, wide - LANES), F32)], axis=1)
    lane = lax.broadcasted_iota(jnp.int32, (blocks, wide), 1)
    row = lax.broadcasted_iota(jnp.int32, (blocks, wide), 0)
    across = jnp.sum(jnp.where(lane - at_exponent == row, exponent, 0.0), axis=0, keepdims=True)
    message = jnp.where(lane < at_energy, force, energy)
    message = jnp.where(lane >= at_exponent, across, message)
    message = jnp.where(lane >= at_old, old_ref[...], message)
    message = jnp.where(lane >= at_kinetic, kinetic, message)
    for k in range(walk * folds):
        c = k % folds
        send_ref[pl.ds(k, blocks, stride=walk * folds), :] = message[:, c * LANES : (c + 1) * LANES]


def finish_kernel(slab, offsets, blocks, walk, got_ref, force_ref, energy_ref, weight_ref, comb_ref):
    folds = got_ref.shape[0] // (blocks * walk)
    wide = folds * LANES
    at_energy, at_exponent, at_old, at_kinetic = offsets
    own_block = lax.axis_index("blk")
    own_walk = lax.axis_index("walk")
    lane = lax.broadcasted_iota(jnp.int32, (blocks, wide), 1)
    row = lax.broadcasted_iota(jnp.int32, (blocks, wide), 0)
    keep = (lane < at_old) | (lane - at_old == row) | (lane - at_kinetic == row)
    own = jnp.zeros((blocks, wide), F32)
    sums = []
    for w in range(walk):
        from_w = [got_ref[pl.ds(w * folds + c, blocks, stride=walk * folds), :] for c in range(folds)]
        from_w = jnp.concatenate(from_w, axis=1)
        own = jnp.where(own_walk == w, from_w, own)
        sums.append(jnp.sum(jnp.where(keep, from_w, 0.0), axis=0, keepdims=True))
    for b in range(blocks):
        force_ref[:, b * slab : (b + 1) * slab] = own[b : b + 1, :slab]
    sums = jnp.concatenate(sums, axis=0)
    place = lax.broadcasted_iota(jnp.int32, (walk, wide), 1) - at_exponent
    inside = (place >= 0) & (place < blocks)
    old = pltpu.roll(sums, wide - (at_old - at_exponent), 1)
    kinetic = pltpu.roll(sums, wide - (at_kinetic - at_exponent), 1)
    change = jnp.where(inside, sums - 0.01 * kinetic, 0.0)
    weight = jnp.where(inside, old * jnp.exp(change), 0.0)
    index = place * walk + lax.broadcasted_iota(jnp.int32, (walk, wide), 0)
    rank = own_block * walk + own_walk

    def total(values):
        return jnp.sum(values, axis=(0, 1), keepdims=True)

    before = total(jnp.where(index < rank, weight, 0.0))
    weight_ref[...] = total(jnp.where(index == rank, weight, 0.0))
    energy_ref[...] = total(jnp.where(lane == at_energy, own, 0.0)) + total(jnp.where(inside & (index == rank), kinetic, 0.0))
    comb_ref[...] = before * (blocks * walk) / total(weight) - rank.astype(F32)


def on_device(green_half, chol_half, one_body, field_noise, old_weight):
    slab, occupied, orbitals = chol_half.shape
    blocks = lax.axis_size("blk")
    walk = lax.axis_size("walk")
    order = exchange_order(blocks)
    vmem = pl.BlockSpec(memory_space=pltpu.VMEM)
    products = plan_of(occupied)[2]
    small = pltpu.CompilerParams(vmem_limit_bytes=4 * 2**20)
    message = (blocks, MESSAGE, LANES)
    packed = pl.pallas_call(
        functools.partial(pack_kernel, slab, order),
        out_shape=jax.ShapeDtypeStruct(message, BF16),
        in_specs=[vmem, vmem],
        out_specs=vmem,
        scratch_shapes=[pltpu.VMEM((2, STRIDE, LANES), F32)],
        compiler_params=pltpu.CompilerParams(vmem_limit_bytes=60 * 2**20),
        name="pack",
    )(green_half, field_noise)
    arrived = lax.all_to_all(packed, "blk", split_axis=0, concat_axis=0, axis_index_groups=[order], tiled=True)
    rhs = pl.pallas_call(
        functools.partial(prepare_kernel, slab),
        out_shape=jax.ShapeDtypeStruct((products, 2 * LANES, orbitals), BF16),
        in_specs=[vmem],
        out_specs=vmem,
        compiler_params=pltpu.CompilerParams(vmem_limit_bytes=12 * 2**20),
        name="prepare",
    )(jnp.swapaxes(chol_half, 0, 1))
    offsets = (slab, slab + 1, slab + 1 + blocks, slab + 1 + 2 * blocks)
    folds = round_up(slab + 1 + 3 * blocks, LANES) // LANES
    send = pl.pallas_call(
        functools.partial(work_kernel, slab, order, offsets, walk),
        out_shape=jax.ShapeDtypeStruct((blocks * walk * folds, LANES), F32),
        in_specs=[vmem] * 4,
        out_specs=vmem,
        scratch_shapes=[
            pltpu.VMEM((round_up(orbitals, LANES) // LANES, GROUP * STRIDE, LANES), F32),
            pltpu.VMEM((GROUP * occupied, orbitals), BF16),
            pltpu.VMEM((products, GROUP * occupied, 2 * LANES), F32),
        ],
        compiler_params=pltpu.CompilerParams(vmem_limit_bytes=32 * 2**20),
        name="work",
    )(arrived, rhs, one_body, old_weight.reshape(1, 1))
    got = lax.all_to_all(send, ("blk", "walk"), split_axis=0, concat_axis=0, tiled=True)
    one = jax.ShapeDtypeStruct((1, 1), F32)
    force, energy, weight, comb = pl.pallas_call(
        functools.partial(finish_kernel, slab, offsets, blocks, walk),
        out_shape=(jax.ShapeDtypeStruct((1, slab * blocks), F32), one, one, one),
        in_specs=[vmem],
        out_specs=(vmem,) * 4,
        compiler_params=small,
        name="finish",
    )(got)
    return force, energy.reshape(1), weight.reshape(1), comb.reshape(1)


def solution(mesh):
    placed = (
        P(("blk", "walk"), None, None),
        P("blk", None, None),
        P(),
        P(("blk", "walk"), None),
        P(("blk", "walk")),
    )
    return jax.shard_map(
        on_device,
        mesh=mesh,
        in_specs=placed,
        out_specs=(
            P(("blk", "walk"), None),
            P(("blk", "walk")),
            P(("blk", "walk")),
            P(("blk", "walk")),
        ),
        check_vma=False,
    )
```
